1024 devices in a mesh: gx: 8 (over z_lo, core), gy: 4 (over x), gz: 32 (over z_hi, y).
Axes of the slice: x: 4, y: 8, z: 16 (z_hi: 4, z_lo: 4; z = z_hi * 4 + z_lo), core: 2. Of those that a mesh axis runs over, the one named last changes fastest.
Arguments:
- rhs: float32 [32, 16, 1024, 512], P('gx', 'gy', 'gz'), may hold values from -6 to 6
- coef: float32 [32, 16, 1024], P('gx', 'gy', 'gz'), may hold values from 1 to 4
- mass: float32 [512, 512], replicated, as said below
- smoother: float32 [512, 512], replicated, as said below
- lift: float32 [384, 512], replicated, may hold values from -0.15 to 0.15
- restrict: float32 [512, 8], replicated, may hold values from -0.25 to 0.25
- coarse_block_matrix: float32 [8, 8], replicated
- element_cluster_index: int32 [32, 16, 1024], P('gx', 'gy', 'gz'), may hold values from 0 to 63
Outputs:
- corrected: float32 [32, 16, 1024, 512], P('gx', 'gy', 'gz')
The draws below stay inside these ranges and needn't reach their ends.
Inputs may be any that keep to these rules, and one draw needn't show every extreme that they name: `element_cluster_index`: index of an agglomerate within the element's own device block. `mass`: identity plus independent entries of deviation 0.15 / sqrt(512). `smoother`: identity minus the off-diagonal part of mass.
All inputs are finite; a program needn't handle non-finite values.
Results may differ from the reference program's by a relative error of at most 0.00005.
Values sent between devices are 32-bit elements; how exact they have to be, the bound alone decides.
A program may use at most 64 MiB of HBM per device.

```python
import math
import jax
import jax.numpy as jnp
from jax import lax

EDGE = 8
ELEMENT_DOFS = 512
FACE = 64
COARSE = 8
EX = 4
EY = 4
EZ = 32
DEVICE_CLUSTERS = 64
ELEMENTS_X = 32
ELEMENTS_Y = 16
ELEMENTS_Z = 1024
N_GX = 8
N_GY = 4
N_GZ = 32


def shared_part(key):
    noise = jax.random.normal(key, (ELEMENT_DOFS, ELEMENT_DOFS), jnp.float32)
    noise = jnp.clip(noise, -5.0, 5.0) * (0.15 / ELEMENT_DOFS ** 0.5)
    return noise * (1.0 - jnp.eye(ELEMENT_DOFS, dtype=jnp.float32))


def draw_mass(key, part):
    offdiag = shared_part(key)
    return jnp.eye(ELEMENT_DOFS, dtype=jnp.float32) + offdiag


def draw_smoother(key, part):
    offdiag = shared_part(key)
    return jnp.eye(ELEMENT_DOFS, dtype=jnp.float32) - offdiag


def draw_coarse_block_matrix(key, part):
    key = jax.random.fold_in(key, 7)
    noise = jnp.clip(jax.random.normal(key, (COARSE, COARSE), jnp.float32), -4.0, 4.0)
    return jnp.eye(COARSE, dtype=jnp.float32) + 0.1 * noise


def set_ends(array, stream_key, smallest, top_value):
    longest = array.shape.index(max(array.shape))
    spots = []
    for shift in (0, 1):
        where = [jax.random.randint(jax.random.fold_in(stream_key, axis), (), 0, length) for axis, length in enumerate(array.shape)]
        where[longest] = (where[longest] + shift) % array.shape[longest]
        spots.append(tuple(where))
    return array.at[spots[0]].set(smallest).at[spots[1]].set(top_value)


def block_levels(own_key, shape, shards, smallest, largest):
    def one(position, shards_of):
        heights = jax.random.uniform(jax.random.fold_in(jax.random.fold_in(own_key, 6), position), (shards_of,), jnp.float32, smallest / len(shards), largest / len(shards))
        return jnp.repeat(jnp.exp(heights), shape[position] // shards_of).reshape((-1,) + (1,) * (len(shape) - position - 1))

    factor_of = one(*shards[0])
    for cut in shards[1:]:
        factor_of = factor_of * one(*cut)
    return factor_of


def centred(rng, dims, spread, most, cuts=(), kind=jnp.bfloat16):
    gain = block_levels(rng, dims, cuts, -0.22, 0.18) if cuts else 1.0
    array = jax.random.normal(rng, dims, jnp.float32) * spread * gain
    return jnp.minimum(jnp.maximum(array, -most), most).astype(kind)


def setup_inputs(seed: int = 0) -> dict:
    arg_keys = jax.random.split(jax.random.key(seed), 9)
    return {
        "rhs": centred(arg_keys[0], (ELEMENTS_X, ELEMENTS_Y, ELEMENTS_Z, ELEMENT_DOFS), 1.0, 6.0, ((0, 8), (1, 4), (2, 32)), jnp.float32),
        "coef": jnp.clip(jnp.exp(math.log(4.0) - 1.3862944 * jax.random.uniform(arg_keys[1], (ELEMENTS_X, ELEMENTS_Y, ELEMENTS_Z), jnp.float32) ** block_levels(arg_keys[1], (ELEMENTS_X, ELEMENTS_Y, ELEMENTS_Z), ((0, 8), (1, 4), (2, 32)), -0.2, 0.2)), 1.0, 4.0),
        "mass": draw_mass(jax.random.fold_in(arg_keys[8], 71), 0),
        "smoother": draw_smoother(jax.random.fold_in(arg_keys[8], 71), 0),
        "lift": centred(arg_keys[4], (6 * FACE, ELEMENT_DOFS), 0.025, 0.15, (), jnp.float32),
        "restrict": centred(arg_keys[5], (ELEMENT_DOFS, COARSE), ELEMENT_DOFS ** -0.5, 0.25, (), jnp.float32),
        "coarse_block_matrix": draw_coarse_block_matrix(jax.random.fold_in(arg_keys[8], 71), 0),
        "element_cluster_index": set_ends(jax.random.randint(arg_keys[7], (ELEMENTS_X, ELEMENTS_Y, ELEMENTS_Z), 0, DEVICE_CLUSTERS), jax.random.fold_in(arg_keys[7], 1), 0, DEVICE_CLUSTERS - 1).astype(jnp.int32),
    }


def face_traces(field):
    cube = field.reshape(field.shape[:-1] + (EDGE, EDGE, EDGE))
    lead = field.shape[:-1]
    last = EDGE - 1
    parts = [cube[..., 0, :, :], cube[..., last, :, :], cube[..., :, 0, :], cube[..., :, last, :], cube[..., :, :, 0], cube[..., :, :, last]]
    return jnp.concatenate([p.reshape(lead + (FACE,)) for p in parts], -1)


def neighbour_faces(padded):
    width = FACE
    return jnp.concatenate([
        padded[:-2, 1:-1, 1:-1, width:2 * width], padded[2:, 1:-1, 1:-1, 0:width],
        padded[1:-1, :-2, 1:-1, 3 * width:4 * width], padded[1:-1, 2:, 1:-1, 2 * width:3 * width],
        padded[1:-1, 1:-1, :-2, 5 * width:6 * width], padded[1:-1, 1:-1, 2:, 4 * width:5 * width]], -1)


def reference(rhs, coef, mass, smoother, lift, restrict, coarse_block_matrix, element_cluster_index):
    high = lax.Precision.HIGHEST

    def mult(a, b):
        return jnp.matmul(a, b, precision=high)

    def operate(field):
        padded = jnp.pad(face_traces(field), ((1, 1), (1, 1), (1, 1), (0, 0)))
        return coef[..., None] * mult(field, mass) - mult(neighbour_faces(padded), lift)

    first = mult(rhs, smoother) / coef[..., None]
    second = first + mult(rhs - operate(first), smoother) / coef[..., None]
    resid = rhs - operate(second)
    small = mult(resid, restrict)
    gxn, gyn, gzn = N_GX, N_GY, N_GZ
    blocks = small.reshape(gxn, EX, gyn, EY, gzn, EZ, COARSE).transpose(2, 4, 0, 1, 3, 5, 6)
    blocks = blocks.reshape(gyn, gzn, gxn, EX * EY * EZ, COARSE)
    labels = element_cluster_index.reshape(gxn, EX, gyn, EY, gzn, EZ).transpose(2, 4, 0, 1, 3, 5)
    labels = labels.reshape(gyn, gzn, gxn, EX * EY * EZ)
    onehot = (labels[..., None] == jnp.arange(DEVICE_CLUSTERS, dtype=jnp.int32)).astype(jnp.float32)
    coarse_rhs = jnp.einsum('yzgea,yzgek->yzkga', onehot, blocks, precision=high).reshape(gyn, gzn, COARSE, gxn * DEVICE_CLUSTERS)
    weight_factor = (1.0 + jnp.sum(onehot, 3)).reshape(gyn, gzn, 1, gxn * DEVICE_CLUSTERS)
    zone = coarse_rhs / weight_factor
    zpad = jnp.pad(zone, ((1, 1), (1, 1), (0, 0), (0, 0)))
    nearby = zpad[:-2, 1:-1] + zpad[2:, 1:-1] + zpad[1:-1, :-2] + zpad[1:-1, 2:]
    line_sum = jnp.sum(zone.reshape(gyn, gzn, COARSE, gxn, DEVICE_CLUSTERS), 3, keepdims=True)
    line_sum = jnp.broadcast_to(line_sum, (gyn, gzn, COARSE, gxn, DEVICE_CLUSTERS)).reshape(zone.shape)
    applied = weight_factor * jnp.einsum('kl,yzla->yzka', coarse_block_matrix, zone, precision=high) - nearby - line_sum
    ztwo = zone + (coarse_rhs - applied) / weight_factor
    ztwo = ztwo.reshape(gyn, gzn, COARSE, gxn, DEVICE_CLUSTERS)
    picked = jnp.einsum('yzgea,yzkga->yzgek', onehot, ztwo, precision=high)
    corr = mult(picked, restrict.T)
    corr = corr.reshape(gyn, gzn, gxn, EX, EY, EZ, ELEMENT_DOFS).transpose(2, 3, 0, 4, 1, 5, 6)
    return second + corr.reshape(second.shape)
```

```python
import functools

import jax
import jax.numpy as jnp
from jax import lax
from jax.experimental import pallas as pl
from jax.experimental.pallas import tpu as pltpu
from jax.sharding import PartitionSpec as P

N = 512
FACE = 64
F32 = jnp.float32
BF16 = jnp.bfloat16
MESH = pl.DeviceIdType.MESH
NT = (((1,), (1,)), ((), ()))
TN = (((0,), (0,)), ((), ()))
NN = (((1,), (0,)), ((), ()))


def dot3(a, b, dims=NN):
    return lax.dot_general(a, b, dims, precision=lax.Precision.HIGH, preferred_element_type=F32)


def halves(a):
    hi = a.astype(BF16)
    return hi, (a - hi.astype(F32)).astype(BF16)


def dot1(a, b):
    return jnp.dot(a, b, preferred_element_type=F32)


def iota(shape, dim):
    return lax.broadcasted_iota(jnp.int32, shape, dim)


def kernel(
    sizes, rhs_hbm, coef_hbm, mass_hbm, smoother_hbm, lift_hbm, restrict_hbm, cbm_hbm, label_hbm,
    out_ref,
    rhs, mass, smoother, lift, restrict, cbm, coef, label,
    dcol, onehot, pick, u, first, tr, faces, big, ls, lsg, g, x_t,
    out_a, in_a, out_z, in_z, in_bx, in_by, in_bz, zone_out, in_zone,
    load_sem, sa, ra, sb, rb, sz, rz,
):
    ngx, ngy, ngz = sizes
    gx, gy, gz = lax.axis_index("gx"), lax.axis_index("gy"), lax.axis_index("gz")

    loads = [
        pltpu.make_async_copy(src, dst, load_sem.at[n])
        for n, (src, dst) in enumerate(
            [
                (rhs_hbm, rhs),
                (smoother_hbm, smoother),
                (coef_hbm, coef),
                (label_hbm, label),
                (restrict_hbm, restrict),
                (cbm_hbm, cbm),
                (mass_hbm, mass),
                (lift_hbm.at[FACE : 2 * FACE], lift.at[0:FACE]),
                (lift_hbm.at[0:FACE], lift.at[FACE : 2 * FACE]),
                (lift_hbm.at[2 * FACE :], lift.at[2 * FACE :]),
            ]
        )
    ]
    for copy in loads:
        copy.start()

    def along(axis, place, size, step):
        return {axis: lax.rem(place + (step + size), size)}

    down = [along("gx", gx, ngx, -1), along("gy", gy, ngy, -1), along("gz", gz, ngz, -1)]
    up = [along("gx", gx, ngx, 1), along("gy", gy, ngy, 1), along("gz", gz, ngz, 1)]
    line = [along("gx", gx, ngx, step) for step in range(1, ngx)]

    barrier = pltpu.get_barrier_semaphore()
    partners = line + down[1:] + up[1:]
    for partner in partners:
        pl.semaphore_signal(barrier, inc=1, device_id=partner, device_id_type=MESH)

    node, face = iota((N, 256), 0), iota((N, 256), 1)
    block, within = face // FACE, face % FACE
    hi, lo = within // 8, within % 8
    end = jnp.where(block % 2 == 0, 7, 0)
    wanted = jnp.where(block < 2, hi * 64 + end * 8 + lo, hi * 64 + lo * 8 + end)
    pick[...] = jnp.where(node == wanted, 1.0, 0.0).astype(BF16)

    lane = iota((32, 128), 1)
    row = iota((32, 128), 0)

    def column(values):
        return jnp.sum(jnp.where(lane == row, jnp.broadcast_to(values, (32, 128)), 0.0), 1, keepdims=True)

    loads[2].wait()
    loads[3].wait()
    pad = jnp.zeros((1, 96), F32)
    for s in range(16):
        values = jnp.concatenate([coef[s // 4, s % 4 : s % 4 + 1, :], pad], 1)
        dcol[32 * s : 32 * s + 32, :] = jnp.broadcast_to(1.0 / column(values), (32, 128))
        names = jnp.concatenate([label[s // 4, s % 4 : s % 4 + 1, :].astype(F32), pad], 1)
        names = jnp.broadcast_to(column(names), (32, 128)).astype(jnp.int32)
        onehot[32 * s : 32 * s + 32, :] = jnp.where(names == lane, 1.0, 0.0)
    d4 = lambda a: jnp.concatenate([a] * 4, 1)

    loads[0].wait()
    loads[1].wait()
    u[...] = dot3(rhs[...], smoother[...])
    first[...] = u[...] * d4(dcol[...])
    f_hi, f_lo = halves(first[...])
    tr[...] = dot1(f_hi, pick[...]) + dot1(f_lo, pick[...])

    low = iota((FACE, 128), 1) < FACE
    swap = lambda a: pltpu.roll(a, FACE, 1)
    top, bottom = first[384:512, 384:512], first[0:128, 0:128]
    out_a[0] = jnp.where(low, swap(top[0:64]), top[64:128])
    out_a[1] = jnp.where(low, bottom[0:64], swap(bottom[64:128]))
    ytop = [tr[128 * i + 96 : 128 * i + 128, 0:128] for i in range(4)]
    ybottom = [tr[128 * i : 128 * i + 32, 0:128] for i in range(4)]
    out_a[2] = jnp.where(low, jnp.concatenate(ytop[:2], 0), swap(jnp.concatenate(ytop[2:], 0)))
    out_a[3] = jnp.where(low, swap(jnp.concatenate(ybottom[:2], 0)), jnp.concatenate(ybottom[2:], 0))
    for s in range(16):
        out_z[0, s : s + 1, :] = tr[32 * s + 31 : 32 * s + 32, 128:256]
        out_z[1, s : s + 1, :] = tr[32 * s : 32 * s + 1, 128:256]

    pl.semaphore_wait(barrier, len(partners))

    def send(src, dst, send_sem, recv_sem, device):
        copy = pltpu.make_async_remote_copy(
            src_ref=src, dst_ref=dst, send_sem=send_sem, recv_sem=recv_sem,
            device_id=device, device_id_type=MESH,
        )
        copy.start()
        return copy

    a_copies = []
    for dim in range(3):
        for way, device in enumerate((up[dim], down[dim])):
            n = 2 * dim + way
            src, dst = (out_a.at[n], in_a.at[n]) if dim < 2 else (out_z.at[way], in_z.at[way])
            a_copies.append(send(src, dst, sa.at[n], ra.at[n], device))

    low32 = lane < FACE
    nothing = jnp.zeros((32, 128), F32)
    for s in range(16):
        x, y = s // 4, s % 4
        rows = slice(32 * s, 32 * s + 32)
        above = first[32 * s + 128 : 32 * s + 160, 0:128] if x < 3 else nothing
        below = first[32 * s - 128 : 32 * s - 96, 384:512] if x > 0 else nothing
        faces[rows, 0:128] = jnp.where(low32, above, below)
        above = tr[32 * s + 32 : 32 * s + 64, 0:128] if y < 3 else nothing
        below = tr[32 * s - 32 : 32 * s, 0:128] if y > 0 else nothing
        faces[rows, 128:256] = jnp.where(low32, below, above)
        own = tr[rows, 128:256]
        below = jnp.where(row == 0, 0.0, pltpu.roll(own, 1, 0))
        above = jnp.where(row == 31, 0.0, pltpu.roll(own, 31, 0))
        faces[rows, 256:384] = jnp.where(low32, below, above)

    for copy in loads[4:]:
        copy.wait()

    many = jnp.concatenate([restrict[...]] * 16, 0)
    lane_n = iota((N, 128), 1)
    lift_r = dot3(lift[...], many, NT)
    face_row = iota((384, 128), 0) // FACE
    lift_r = jnp.where(iota((384, 128), 1) // 8 == face_row + 1, lift_r, 0.0)
    g_now = jnp.where(lane_n < 8, dot3(mass[...], many, NT), 0.0)
    l_hi, l_lo = halves(lift_r[128:384])
    g_now = g_now + (dot1(pick[...], l_hi) + dot1(pick[...], l_lo))
    g[...] = g_now
    g[0:64, :] = g[0:64, :] + lift_r[0:64]
    g[448:512, :] = g[448:512, :] + lift_r[64:128]
    ls[...] = dot3(lift[...], smoother[...])
    lsg[...] = dot3(ls[...], g[...])
    rr = dot3(rhs[...], many, NT)

    big[...] = rhs[...] - dot3(u[...], mass[...]) + dot3(faces[...], lift[...])
    u[...] = u[...] + dot3(big[...], smoother[...])
    w = dot3(u[...], g[...])
    x_t[...] = w

    for copy in a_copies:
        copy.wait_recv()
    is_in = [
        jnp.where(gx > 0, 1.0, 0.0), jnp.where(gx < ngx - 1, 1.0, 0.0),
        jnp.where(gy > 0, 1.0, 0.0), jnp.where(gy < ngy - 1, 1.0, 0.0),
        jnp.where(gz > 0, 1.0, 0.0), jnp.where(gz < ngz - 1, 1.0, 0.0),
    ]
    halo_rows = []
    for n in range(4):
        packed = in_a[n] * is_in[n]
        halo = jnp.concatenate([packed, swap(packed)], 0)[:, 0:FACE]
        at = {0: 64, 1: 0, 2: 128, 3: 192}[n]
        halo_rows.append((n, halo, at))
        add = dot3(halo, lsg[at : at + FACE, :])
        if n == 0:
            x_t[0:128, :] = x_t[0:128, :] + add
        elif n == 1:
            x_t[384:512, :] = x_t[384:512, :] + add
        else:
            for i in range(4):
                j = 128 * i + (0 if n == 2 else 96)
                x_t[j : j + 32, :] = x_t[j : j + 32, :] + add[32 * i : 32 * i + 32]
    z_low = in_z[0] * is_in[4]
    z_high = in_z[1] * is_in[5]
    add_low = dot3(z_low[:, 0:FACE], lsg[256:320, :])
    add_high = dot3(z_high[:, FACE:128], lsg[320:384, :])
    for s in range(16):
        x_t[32 * s : 32 * s + 1, :] = x_t[32 * s : 32 * s + 1, :] + add_low[s : s + 1]
        x_t[32 * s + 31 : 32 * s + 32, :] = x_t[32 * s + 31 : 32 * s + 32, :] + add_high[s : s + 1]

    w = x_t[...]
    w = jnp.where(lane_n < 8, rr - w, w * dcol[...])
    c = big
    c[0:128, :] = w.T

    b_copies = [
        send(c.at[16:24, 384:512], in_bx.at[0], sb.at[0], rb.at[0], up[0]),
        send(c.at[8:16, 0:128], in_bx.at[1], sb.at[1], rb.at[1], down[0]),
        send(c.at[24:32, :], in_by.at[0], sb.at[2], rb.at[2], up[1]),
        send(c.at[32:40, :], in_by.at[1], sb.at[3], rb.at[3], down[1]),
        send(c.at[40:48, :], in_bz.at[0], sb.at[4], rb.at[4], up[2]),
        send(c.at[48:56, :], in_bz.at[1], sb.at[5], rb.at[5], down[2]),
    ]

    small = c[0:8, :]
    none8 = jnp.zeros((8, 128), F32)
    place = iota((8, N), 1)
    py, pz = (place // 32) % 4, place % 32
    small = small + jnp.concatenate([c[8:16, 128:512], none8], 1)
    small = small + jnp.concatenate([none8, c[16:24, 0:384]], 1)
    small = small + jnp.where(py > 0, pltpu.roll(c[24:32, :], 32, 1), 0.0)
    small = small + jnp.where(py < 3, pltpu.roll(c[32:40, :], N - 32, 1), 0.0)
    small = small + jnp.where(pz > 0, pltpu.roll(c[40:48, :], 1, 1), 0.0)
    small = small + jnp.where(pz < 31, pltpu.roll(c[48:56, :], N - 1, 1), 0.0)
    weight = 1.0 + jnp.sum(onehot[...], 0, keepdims=True)
    weight = jnp.broadcast_to(weight, (8, 128))

    for copy in b_copies:
        copy.wait_recv()
    zeros_mid = jnp.zeros((8, 256), F32)
    small = small + jnp.concatenate([in_bx[0] * is_in[0], zeros_mid, in_bx[1] * is_in[1]], 1)
    small = small + jnp.where(py == 0, pltpu.roll(in_by[0], N - 96, 1) * is_in[2], 0.0)
    small = small + jnp.where(py == 3, pltpu.roll(in_by[1], 96, 1) * is_in[3], 0.0)
    small = small + jnp.where(pz == 0, pltpu.roll(in_bz[0], N - 31, 1) * is_in[4], 0.0)
    small = small + jnp.where(pz == 31, pltpu.roll(in_bz[1], 31, 1) * is_in[5], 0.0)
    coarse_rhs = dot3(small, onehot[...])
    zone = coarse_rhs / weight
    zone_out[...] = zone

    z_copies = []
    for n, device in enumerate(line + [up[1], down[1], up[2], down[2]]):
        z_copies.append(send(zone_out, in_zone.at[n], sz.at[n], rz.at[n], device))

    add_low = dot3(z_low[:, 0:FACE], ls[256:320, :])
    add_high = dot3(z_high[:, FACE:128], ls[320:384, :])
    for s in range(16):
        u[32 * s : 32 * s + 1, :] = u[32 * s : 32 * s + 1, :] + add_low[s : s + 1]
        u[32 * s + 31 : 32 * s + 32, :] = u[32 * s + 31 : 32 * s + 32, :] + add_high[s : s + 1]
    for n, halo, at in halo_rows:
        add = dot3(halo, ls[at : at + FACE, :])
        if n == 0:
            u[0:128, :] = u[0:128, :] + add
        elif n == 1:
            u[384:512, :] = u[384:512, :] + add
        else:
            for i in range(4):
                j = 128 * i + (0 if n == 2 else 96)
                u[j : j + 32, :] = u[j : j + 32, :] + add[32 * i : 32 * i + 32]
    u[...] = u[...] * d4(dcol[...])
    inner = weight * dot3(cbm[...], zone)

    for copy in z_copies:
        copy.wait_recv()
    total = zone
    for n in range(ngx - 1):
        total = total + in_zone[n]
    k = ngx - 1
    total = total + (in_zone[k] * is_in[2] + in_zone[k + 1] * is_in[3] + in_zone[k + 2] * is_in[4] + in_zone[k + 3] * is_in[5])
    two = zone + (coarse_rhs - (inner - total)) / weight
    spread = dot3(two, restrict[...], TN)
    s_hi, s_lo = halves(spread)
    one = onehot[...].astype(BF16)
    out_ref[...] = u[...] + (dot1(one, s_hi) + dot1(one, s_lo))

    for copy in a_copies + b_copies + z_copies:
        copy.wait_send()


def shards(sizes, rhs, coef, mass, smoother, lift, restrict, coarse_block_matrix, element_cluster_index):
    others = sizes[0] - 1 + 4
    hbm = pl.BlockSpec(memory_space=pl.ANY)
    dma = pltpu.SemaphoreType.DMA
    out = pl.pallas_call(
        functools.partial(kernel, sizes),
        out_shape=jax.ShapeDtypeStruct((N, N), F32),
        in_specs=[hbm] * 8,
        out_specs=pl.BlockSpec(memory_space=pltpu.VMEM),
        scratch_shapes=[
            pltpu.VMEM((N, N), F32),
            pltpu.VMEM((N, N), F32),
            pltpu.VMEM((N, N), F32),
            pltpu.VMEM((384, N), F32),
            pltpu.VMEM((8, N), F32),
            pltpu.VMEM((8, 8), F32),
            pltpu.VMEM((4, 4, 32), F32),
            pltpu.VMEM((4, 4, 32), jnp.int32),
            pltpu.VMEM((N, 128), F32),
            pltpu.VMEM((N, 128), F32),
            pltpu.VMEM((N, 256), BF16),
            pltpu.VMEM((N, N), F32),
            pltpu.VMEM((N, N), F32),
            pltpu.VMEM((N, 256), F32),
            pltpu.VMEM((N, 384), F32),
            pltpu.VMEM((N, N), F32),
            pltpu.VMEM((384, N), F32),
            pltpu.VMEM((384, 128), F32),
            pltpu.VMEM((N, 128), F32),
            pltpu.VMEM((N, 128), F32),
            pltpu.VMEM((4, 64, 128), F32),
            pltpu.VMEM((4, 64, 128), F32),
            pltpu.VMEM((2, 16, 128), F32),
            pltpu.VMEM((2, 16, 128), F32),
            pltpu.VMEM((2, 8, 128), F32),
            pltpu.VMEM((2, 8, N), F32),
            pltpu.VMEM((2, 8, N), F32),
            pltpu.VMEM((8, 128), F32),
            pltpu.VMEM((others, 8, 128), F32),
            dma((10,)),
            dma((6,)),
            dma((6,)),
            dma((6,)),
            dma((6,)),
            dma((others,)),
            dma((others,)),
        ],
        compiler_params=pltpu.CompilerParams(
            collective_id=0, has_side_effects=True, vmem_limit_bytes=40 * 1024 * 1024
        ),
        name="cycle",
    )(rhs.reshape(N, N), coef, mass, smoother, lift, restrict.T, coarse_block_matrix, element_cluster_index)
    return out.reshape(rhs.shape)


def solution(mesh):
    sizes = tuple(mesh.shape[a] for a in ("gx", "gy", "gz"))
    return jax.shard_map(
        functools.partial(shards, sizes),
        mesh=mesh,
        in_specs=(
            P("gx", "gy", "gz", None),
            P("gx", "gy", "gz"),
            P(),
            P(),
            P(),
            P(),
            P(),
            P("gx", "gy", "gz"),
        ),
        out_specs=P("gx", "gy", "gz", None),
        check_vma=False,
    )
```

```python
import functools

import jax
import jax.numpy as jnp
from jax import lax
from jax.experimental import pallas as pl
from jax.experimental.pallas import tpu as pltpu
from jax.sharding import PartitionSpec as P

N = 512
FACE = 64
F32 = jnp.float32
BF16 = jnp.bfloat16
MESH = pl.DeviceIdType.MESH
NT = (((1,), (1,)), ((), ()))
TN = (((0,), (0,)), ((), ()))
NN = (((1,), (0,)), ((), ()))


def dot3(a, b, dims=NN):
    return lax.dot_general(a, b, dims, precision=lax.Precision.HIGH, preferred_element_type=F32)


def halves(a):
    hi = a.astype(BF16)
    return hi, (a - hi.astype(F32)).astype(BF16)


def dot1(a, b):
    return jnp.dot(a, b, preferred_element_type=F32)


def iota(shape, dim):
    return lax.broadcasted_iota(jnp.int32, shape, dim)


def kernel(
    sizes, rhs_hbm, coef_hbm, mass_hbm, smoother_hbm, lift_hbm, restrict_hbm, cbm_hbm, label_hbm,
    out_ref,
    rhs, mass, smoother, lift, restrict, cbm, coef, label,
    dcol, onehot, pick, u, first, tr, faces, v, g_cat, g_top,
    out_a, in_a, out_z, in_z, c, in_bx, in_by, in_bz, zone_out, in_zone,
    load_sem, sa, ra, sb, rb, sz, rz,
):
    ngx, ngy, ngz = sizes
    places = [lax.axis_index(axis) for axis in ("gx", "gy", "gz")]

    loads = [
        pltpu.make_async_copy(src, dst, load_sem.at[n])
        for n, (src, dst) in enumerate(
            [
                (coef_hbm, coef),
                (label_hbm, label),
                (rhs_hbm, rhs),
                (smoother_hbm, smoother),
                (restrict_hbm, restrict),
                (cbm_hbm, cbm),
                (mass_hbm, mass),
                (lift_hbm.at[FACE : 2 * FACE], lift.at[0:FACE]),
                (lift_hbm.at[0:FACE], lift.at[FACE : 2 * FACE]),
                (lift_hbm.at[2 * FACE :], lift.at[2 * FACE :]),
            ]
        )
    ]
    for copy in loads:
        copy.start()

    def along(dim, step):
        size = sizes[dim]
        return {("gx", "gy", "gz")[dim]: lax.rem(places[dim] + (step + size), size)}

    beside = [(along(dim, 1), along(dim, -1)) for dim in range(3)]
    there = [(places[dim] < sizes[dim] - 1, places[dim] > 0) for dim in range(3)]
    line = [along(0, step) for step in range(1, ngx)]

    barrier = pltpu.get_barrier_semaphore()
    for device in line:
        pl.semaphore_signal(barrier, inc=1, device_id=device, device_id_type=MESH)
    partners = ngx - 1
    for dim in (1, 2):
        for way in (0, 1):
            partners = partners + jnp.where(there[dim][way], 1, 0)

            @pl.when(there[dim][way])
            def _():
                pl.semaphore_signal(barrier, inc=1, device_id=beside[dim][way], device_id_type=MESH)

    class Message:
        def __init__(self, src, dst, send_sem, recv_sem, device, goes, comes):
            self.copy = pltpu.make_async_remote_copy(
                src_ref=src, dst_ref=dst, send_sem=send_sem, recv_sem=recv_sem,
                device_id=device, device_id_type=MESH,
            )
            self.goes, self.comes = goes, comes

        def start(self):
            self.when(self.goes, self.copy.start)
            return self

        def wait_recv(self):
            self.when(self.comes, self.copy.wait_recv)

        def wait_send(self):
            self.when(self.goes, self.copy.wait_send)

        def when(self, condition, act):
            if condition is None:
                act()
            else:
                pl.when(condition)(act)

    def shifted(dim, way, src, dst, send_sem, recv_sem):
        return Message(src, dst, send_sem, recv_sem, beside[dim][way], there[dim][way], there[dim][1 - way])

    for dim in range(3):
        for way in (0, 1):

            @pl.when(jnp.logical_not(there[dim][1 - way]))
            def _():
                if dim < 2:
                    in_a[2 * dim + way] = jnp.zeros((FACE, 128), F32)
                else:
                    in_z[way] = jnp.zeros((16, 128), F32)
                if dim == 0:
                    in_bx[way] = jnp.zeros((8, 128), F32)
                elif dim == 1:
                    in_by[way] = jnp.zeros((8, N), F32)
                else:
                    in_bz[way] = jnp.zeros((8, N), F32)
                if dim > 0:
                    in_zone[ngx - 1 + 2 * (dim - 1) + way] = jnp.zeros((8, 128), F32)

    node, face = iota((N, 256), 0), iota((N, 256), 1)
    block, within = face // FACE, face % FACE
    hi, lo = within // 8, within % 8
    end = jnp.where(block % 2 == 0, 7, 0)
    wanted = jnp.where(block < 2, hi * 64 + end * 8 + lo, hi * 64 + lo * 8 + end)
    pick[...] = jnp.where(node == wanted, 1.0, 0.0).astype(BF16)

    lane = iota((32, 128), 1)
    row = iota((32, 128), 0)

    def column(values):
        return jnp.sum(jnp.where(lane == row, jnp.broadcast_to(values, (32, 128)), 0.0), 1, keepdims=True)

    loads[0].wait()
    loads[1].wait()
    pad = jnp.zeros((1, 96), F32)
    for s in range(16):
        values = jnp.concatenate([coef[s // 4, s % 4 : s % 4 + 1, :], pad], 1)
        dcol[32 * s : 32 * s + 32, :] = jnp.broadcast_to(1.0 / column(values), (32, 128))
        names = jnp.concatenate([label[s // 4, s % 4 : s % 4 + 1, :].astype(F32), pad], 1)
        names = jnp.broadcast_to(column(names), (32, 128)).astype(jnp.int32)
        onehot[32 * s : 32 * s + 32, :] = jnp.where(names == lane % 64, 1.0, 0.0)
    d4 = lambda a: jnp.concatenate([a] * 4, 1)

    loads[2].wait()
    loads[3].wait()
    u[...] = dot3(rhs[...], smoother[...])
    first[...] = u[...] * d4(dcol[...])

    low = iota((FACE, 128), 1) < FACE
    swap = lambda a: pltpu.roll(a, FACE, 1)
    top, bottom = first[384:512, 384:512], first[0:128, 0:128]
    out_a[0] = jnp.where(low, swap(top[0:64]), top[64:128])
    out_a[1] = jnp.where(low, bottom[0:64], swap(bottom[64:128]))
    pl.semaphore_wait(barrier, partners)
    a_copies = [
        shifted(0, way, out_a.at[way], in_a.at[way], sa.at[way], ra.at[way]).start() for way in (0, 1)
    ]

    f_hi, f_lo = halves(first[...])
    tr[...] = dot1(f_hi, pick[...]) + dot1(f_lo, pick[...])
    ytop = [tr[128 * i + 96 : 128 * i + 128, 0:128] for i in range(4)]
    ybottom = [tr[128 * i : 128 * i + 32, 0:128] for i in range(4)]
    out_a[2] = jnp.where(low, jnp.concatenate(ytop[:2], 0), swap(jnp.concatenate(ytop[2:], 0)))
    out_a[3] = jnp.where(low, swap(jnp.concatenate(ybottom[:2], 0)), jnp.concatenate(ybottom[2:], 0))
    for s in range(16):
        out_z[0, s : s + 1, :] = tr[32 * s + 31 : 32 * s + 32, 128:256]
        out_z[1, s : s + 1, :] = tr[32 * s : 32 * s + 1, 128:256]
    a_copies += [
        shifted(1, way, out_a.at[2 + way], in_a.at[2 + way], sa.at[2 + way], ra.at[2 + way]).start()
        for way in (0, 1)
    ]
    a_copies += [
        shifted(2, way, out_z.at[way], in_z.at[way], sa.at[4 + way], ra.at[4 + way]).start()
        for way in (0, 1)
    ]

    for copy in loads[4:]:
        copy.wait()

    v[...] = rhs[...] - dot3(u[...], mass[...])

    many = jnp.concatenate([restrict[...]] * 16, 0)
    lane_n = iota((N, 128), 1)
    first_half = lane_n < 64
    kind = (iota((384, 128), 1) % 64) // 8
    lift_r = jnp.where(kind == iota((384, 128), 0) // FACE + 1, dot3(lift[...], many, NT), 0.0)
    g = jnp.where(lane_n % 64 < 8, -dot3(mass[...], many, NT), 0.0)
    l_hi, l_lo = halves(lift_r[128:384])
    g = g + (dot1(pick[...], l_hi) + dot1(pick[...], l_lo))
    g = g + jnp.concatenate([lift_r[0:64], jnp.zeros((384, 128), F32), lift_r[64:128]], 0)
    g_hi, g_lo = halves(g)
    g_cat[...] = jnp.where(first_half, g_hi, g_lo)
    g_top[...] = jnp.where(first_half, g_hi, jnp.zeros_like(g_hi))
    rr = dot3(restrict[...], rhs[...], NT)
    weight = 1.0 + jnp.sum(onehot[...], 0, keepdims=True)
    weight = jnp.broadcast_to(weight, (8, 128))
    per = 1.0 / weight
    d_row = 1.0 / jnp.concatenate([coef[s // 4, s % 4 : s % 4 + 1, :] for s in range(16)], 1)

    low32 = lane < FACE
    nothing = jnp.zeros((32, 128), F32)
    for s in range(16):
        x, y = s // 4, s % 4
        rows = slice(32 * s, 32 * s + 32)
        above = first[32 * s + 128 : 32 * s + 160, 0:128] if x < 3 else nothing
        below = first[32 * s - 128 : 32 * s - 96, 384:512] if x > 0 else nothing
        faces[rows, 0:128] = jnp.where(low32, above, below)
        above = tr[32 * s + 32 : 32 * s + 64, 0:128] if y < 3 else nothing
        below = tr[32 * s - 32 : 32 * s, 0:128] if y > 0 else nothing
        faces[rows, 128:256] = jnp.where(low32, below, above)

    for copy in a_copies:
        copy.wait_recv()
    faces[0:64, 0:128] = jnp.where(low, faces[0:64, 0:128], swap(in_a[0]))
    faces[64:128, 0:128] = jnp.where(low, faces[64:128, 0:128], in_a[0])
    faces[384:448, 0:128] = jnp.where(low, in_a[1], faces[384:448, 0:128])
    faces[448:512, 0:128] = jnp.where(low, swap(in_a[1]), faces[448:512, 0:128])
    for i in range(4):
        half = slice(32 * (i % 2), 32 * (i % 2) + 32)
        below, above = in_a[2, half, :], in_a[3, half, :]
        below = below if i < 2 else swap(below)
        above = swap(above) if i < 2 else above
        j = 128 * i
        faces[j : j + 32, 128:256] = jnp.where(low32, below, faces[j : j + 32, 128:256])
        j = 128 * i + 96
        faces[j : j + 32, 128:256] = jnp.where(low32, faces[j : j + 32, 128:256], above)
    for s in range(16):
        own = tr[32 * s : 32 * s + 32, 128:256]
        below = jnp.where(row == 0, jnp.broadcast_to(in_z[0, s : s + 1, :], (32, 128)), pltpu.roll(own, 1, 0))
        above = jnp.where(row == 31, jnp.broadcast_to(in_z[1, s : s + 1, :], (32, 128)), pltpu.roll(own, 31, 0))
        faces[32 * s : 32 * s + 32, 256:384] = jnp.where(low32, below, above)

    v[...] = v[...] + dot3(faces[...], lift[...])
    u[...] = u[...] + dot3(v[...], smoother[...])
    s_hi, s_lo = halves(u[...])
    w = (dot1(s_hi, g_cat[...]) + dot1(s_lo, g_top[...])).T
    w = w[0:64] + w[64:128]
    c[...] = jnp.concatenate([w[0:8] + rr, w[8:64] * d_row], 0)

    b_copies = [
        shifted(0, 0, c.at[16:24, 384:512], in_bx.at[0], sb.at[0], rb.at[0]).start(),
        shifted(0, 1, c.at[8:16, 0:128], in_bx.at[1], sb.at[1], rb.at[1]).start(),
        shifted(1, 0, c.at[24:32, :], in_by.at[0], sb.at[2], rb.at[2]).start(),
        shifted(1, 1, c.at[32:40, :], in_by.at[1], sb.at[3], rb.at[3]).start(),
        shifted(2, 0, c.at[40:48, :], in_bz.at[0], sb.at[4], rb.at[4]).start(),
        shifted(2, 1, c.at[48:56, :], in_bz.at[1], sb.at[5], rb.at[5]).start(),
    ]
    first[...] = u[...] * d4(dcol[...])

    small = c[0:8, :]
    none8 = jnp.zeros((8, 128), F32)
    place = iota((8, N), 1)
    py, pz = (place // 32) % 4, place % 32
    small = small + jnp.concatenate([c[8:16, 128:512], none8], 1)
    small = small + jnp.concatenate([none8, c[16:24, 0:384]], 1)
    small = small + jnp.where(py > 0, pltpu.roll(c[24:32, :], 32, 1), 0.0)
    small = small + jnp.where(py < 3, pltpu.roll(c[32:40, :], N - 32, 1), 0.0)
    small = small + jnp.where(pz > 0, pltpu.roll(c[40:48, :], 1, 1), 0.0)
    small = small + jnp.where(pz < 31, pltpu.roll(c[48:56, :], N - 1, 1), 0.0)
    one = onehot[...].astype(BF16)
    r_hi, r_lo = halves(restrict[...])
    r_hi, r_lo = r_hi.astype(F32), r_lo.astype(F32)
    r_stack = jnp.concatenate([r_hi, r_hi, r_lo], 0).astype(BF16)

    for copy in b_copies:
        copy.wait_recv()
    zeros_mid = jnp.zeros((8, 256), F32)
    small = small + jnp.concatenate([in_bx[0], zeros_mid, in_bx[1]], 1)
    small = small + jnp.where(py == 0, pltpu.roll(in_by[0], N - 96, 1), 0.0)
    small = small + jnp.where(py == 3, pltpu.roll(in_by[1], 96, 1), 0.0)
    small = small + jnp.where(pz == 0, pltpu.roll(in_bz[0], N - 31, 1), 0.0)
    small = small + jnp.where(pz == 31, pltpu.roll(in_bz[1], 31, 1), 0.0)
    m_hi, m_lo = halves(small)
    parts = dot1(jnp.concatenate([m_hi.astype(F32), m_lo.astype(F32)], 0).astype(BF16), one)
    coarse_rhs = parts[0:8] + parts[8:16]
    zone = coarse_rhs * per
    zone_out[...] = zone

    z_copies = [
        Message(zone_out, in_zone.at[n], sz.at[n], rz.at[n], device, None, None).start()
        for n, device in enumerate(line)
    ]
    for dim in (1, 2):
        for way in (0, 1):
            n = ngx - 1 + 2 * (dim - 1) + way
            z_copies.append(shifted(dim, way, zone_out, in_zone.at[n], sz.at[n], rz.at[n]).start())

    two = zone + (coarse_rhs - (weight * dot3(cbm[...], zone) - zone)) * per

    for copy in z_copies:
        copy.wait_recv()
    total = in_zone[0]
    for n in range(1, ngx + 3):
        total = total + in_zone[n]
    two = two + total * per
    t_hi, t_lo = halves(two)
    t_hi, t_lo = t_hi.astype(F32), t_lo.astype(F32)
    t_stack = jnp.concatenate([t_hi, t_lo, t_hi], 0).astype(BF16)
    spread = lax.dot_general(t_stack, r_stack, TN, preferred_element_type=F32)
    e_hi, e_lo = halves(spread)
    spread = jnp.where(iota((128, N), 0) < 64, e_hi, e_lo)
    out_ref[...] = first[...] + dot1(one, spread)

    for copy in a_copies + b_copies + z_copies:
        copy.wait_send()


def shards(sizes, rhs, coef, mass, smoother, lift, restrict, coarse_block_matrix, element_cluster_index):
    others = sizes[0] - 1 + 4
    hbm = pl.BlockSpec(memory_space=pl.ANY)
    dma = pltpu.SemaphoreType.DMA
    out = pl.pallas_call(
        functools.partial(kernel, sizes),
        out_shape=jax.ShapeDtypeStruct((N, N), F32),
        in_specs=[hbm] * 8,
        out_specs=pl.BlockSpec(memory_space=pltpu.VMEM),
        scratch_shapes=[
            pltpu.VMEM((N, N), F32),
            pltpu.VMEM((N, N), F32),
            pltpu.VMEM((N, N), F32),
            pltpu.VMEM((384, N), F32),
            pltpu.VMEM((8, N), F32),
            pltpu.VMEM((8, 8), F32),
            pltpu.VMEM((4, 4, 32), F32),
            pltpu.VMEM((4, 4, 32), jnp.int32),
            pltpu.VMEM((N, 128), F32),
            pltpu.VMEM((N, 128), F32),
            pltpu.VMEM((N, 256), BF16),
            pltpu.VMEM((N, N), F32),
            pltpu.VMEM((N, N), F32),
            pltpu.VMEM((N, 256), F32),
            pltpu.VMEM((N, 384), F32),
            pltpu.VMEM((N, N), F32),
            pltpu.VMEM((N, 128), BF16),
            pltpu.VMEM((N, 128), BF16),
            pltpu.VMEM((4, FACE, 128), F32),
            pltpu.VMEM((4, FACE, 128), F32),
            pltpu.VMEM((2, 16, 128), F32),
            pltpu.VMEM((2, 16, 128), F32),
            pltpu.VMEM((FACE, N), F32),
            pltpu.VMEM((2, 8, 128), F32),
            pltpu.VMEM((2, 8, N), F32),
            pltpu.VMEM((2, 8, N), F32),
            pltpu.VMEM((8, 128), F32),
            pltpu.VMEM((others, 8, 128), F32),
            dma((10,)),
            dma((6,)),
            dma((6,)),
            dma((6,)),
            dma((6,)),
            dma((others,)),
            dma((others,)),
        ],
        compiler_params=pltpu.CompilerParams(
            collective_id=0, has_side_effects=True, vmem_limit_bytes=62 * 1024 * 1024
        ),
        name="cycle",
    )(rhs.reshape(N, N), coef, mass, smoother, lift, restrict.T, coarse_block_matrix, element_cluster_index)
    return out.reshape(rhs.shape)


def solution(mesh):
    sizes = tuple(mesh.shape[a] for a in ("gx", "gy", "gz"))
    return jax.shard_map(
        functools.partial(shards, sizes),
        mesh=mesh,
        in_specs=(
            P("gx", "gy", "gz", None),
            P("gx", "gy", "gz"),
            P(),
            P(),
            P(),
            P(),
            P(),
            P("gx", "gy", "gz"),
        ),
        out_specs=P("gx", "gy", "gz", None),
        check_vma=False,
    )
```

```python
import functools

import jax
import jax.numpy as jnp
from jax import lax
from jax.experimental import pallas as pl
from jax.experimental.pallas import tpu as pltpu
from jax.sharding import PartitionSpec as P

N = 512
FACE = 64
F32 = jnp.float32
BF16 = jnp.bfloat16
MESH = pl.DeviceIdType.MESH
NT = (((1,), (1,)), ((), ()))
TN = (((0,), (0,)), ((), ()))
NN = (((1,), (0,)), ((), ()))


def dot3(a, b, dims=NN):
    return lax.dot_general(a, b, dims, precision=lax.Precision.HIGH, preferred_element_type=F32)


def halves(a):
    hi = a.astype(BF16)
    return hi, (a - hi.astype(F32)).astype(BF16)


def dot1(a, b):
    return jnp.dot(a, b, preferred_element_type=F32)


def iota(shape, dim):
    return lax.broadcasted_iota(jnp.int32, shape, dim)


def kernel(
    sizes, rhs_hbm, coef_hbm, mass_hbm, smoother_hbm, lift_hbm, restrict_hbm, cbm_hbm, label_hbm,
    out_ref,
    rhs, mass, smoother, lift, restrict, cbm, coef, label,
    dcol, onehot, pick, u, first, tr, faces, v, g_cat, g_top, lz, lzg, wide, rows_z,
    out_a, in_a, out_z, in_z, c, in_bx, in_by, in_bz, zone_out, in_zone,
    load_sem, sa, ra, sb, rb, sz, rz,
):
    ngx, ngy, ngz = sizes
    places = [lax.axis_index(axis) for axis in ("gx", "gy", "gz")]

    loads = [
        pltpu.make_async_copy(src, dst, load_sem.at[n])
        for n, (src, dst) in enumerate(
            [
                (coef_hbm, coef),
                (label_hbm, label),
                (rhs_hbm, rhs),
                (smoother_hbm, smoother),
                (restrict_hbm, restrict),
                (cbm_hbm, cbm),
                (mass_hbm, mass),
                (lift_hbm.at[FACE : 2 * FACE], lift.at[0:FACE]),
                (lift_hbm.at[0:FACE], lift.at[FACE : 2 * FACE]),
                (lift_hbm.at[2 * FACE :], lift.at[2 * FACE :]),
            ]
        )
    ]
    for copy in loads:
        copy.start()

    def along(dim, step):
        size = sizes[dim]
        return {("gx", "gy", "gz")[dim]: lax.rem(places[dim] + (step + size), size)}

    beside = [(along(dim, 1), along(dim, -1)) for dim in range(3)]
    there = [(places[dim] < sizes[dim] - 1, places[dim] > 0) for dim in range(3)]
    line = [along(0, step) for step in range(1, ngx)]

    barrier = pltpu.get_barrier_semaphore()
    for device in line:
        pl.semaphore_signal(barrier, inc=1, device_id=device, device_id_type=MESH)
    partners = ngx - 1
    for dim in (1, 2):
        for way in (0, 1):
            partners = partners + jnp.where(there[dim][way], 1, 0)

            @pl.when(there[dim][way])
            def _():
                pl.semaphore_signal(barrier, inc=1, device_id=beside[dim][way], device_id_type=MESH)

    class Message:
        def __init__(self, src, dst, send_sem, recv_sem, device, goes, comes):
            self.copy = pltpu.make_async_remote_copy(
                src_ref=src, dst_ref=dst, send_sem=send_sem, recv_sem=recv_sem,
                device_id=device, device_id_type=MESH,
            )
            self.goes, self.comes = goes, comes

        def start(self):
            self.when(self.goes, self.copy.start)
            return self

        def wait_recv(self):
            self.when(self.comes, self.copy.wait_recv)

        def wait_send(self):
            self.when(self.goes, self.copy.wait_send)

        def when(self, condition, act):
            if condition is None:
                act()
            else:
                pl.when(condition)(act)

    def shifted(dim, way, src, dst, send_sem, recv_sem):
        return Message(src, dst, send_sem, recv_sem, beside[dim][way], there[dim][way], there[dim][1 - way])

    for dim in range(3):
        for way in (0, 1):

            @pl.when(jnp.logical_not(there[dim][1 - way]))
            def _():
                if dim < 2:
                    in_a[2 * dim + way] = jnp.zeros((FACE, 128), F32)
                else:
                    in_z[way] = jnp.zeros((16, 128), F32)
                if dim == 0:
                    in_bx[way] = jnp.zeros((8, 128), F32)
                elif dim == 1:
                    in_by[way] = jnp.zeros((8, N), F32)
                else:
                    in_bz[way] = jnp.zeros((8, N), F32)
                if dim > 0:
                    in_zone[ngx - 1 + 2 * (dim - 1) + way] = jnp.zeros((8, 128), F32)

    node, face = iota((N, 256), 0), iota((N, 256), 1)
    block, within = face // FACE, face % FACE
    hi, lo = within // 8, within % 8
    end = jnp.where(block % 2 == 0, 7, 0)
    wanted = jnp.where(block < 2, hi * 64 + end * 8 + lo, hi * 64 + lo * 8 + end)
    pick[...] = jnp.where(node == wanted, 1.0, 0.0).astype(BF16)

    lane = iota((32, 128), 1)
    row = iota((32, 128), 0)

    def column(values):
        return jnp.sum(jnp.where(lane == row, jnp.broadcast_to(values, (32, 128)), 0.0), 1, keepdims=True)

    loads[0].wait()
    loads[1].wait()
    pad = jnp.zeros((1, 96), F32)
    for s in range(16):
        values = jnp.concatenate([coef[s // 4, s % 4 : s % 4 + 1, :], pad], 1)
        dcol[32 * s : 32 * s + 32, :] = jnp.broadcast_to(1.0 / column(values), (32, 128))
        names = jnp.concatenate([label[s // 4, s % 4 : s % 4 + 1, :].astype(F32), pad], 1)
        names = jnp.broadcast_to(column(names), (32, 128)).astype(jnp.int32)
        onehot[32 * s : 32 * s + 32, :] = jnp.where(names == lane % 64, 1.0, 0.0)
    d4 = lambda a: jnp.concatenate([a] * 4, 1)

    loads[2].wait()
    loads[3].wait()
    u[...] = dot3(rhs[...], smoother[...])
    first[...] = u[...] * d4(dcol[...])

    for s in range(16):
        rows_z[s : s + 1, :] = first[32 * s + 31 : 32 * s + 32, :]
        rows_z[16 + s : 17 + s, :] = first[32 * s : 32 * s + 1, :]
    ends = rows_z[...]
    e_hi, e_lo = halves(ends)
    ends = dot1(e_hi, pick[:, 128:256]) + dot1(e_lo, pick[:, 128:256])
    out_z[0] = ends[0:16]
    out_z[1] = ends[16:32]
    pl.semaphore_wait(barrier, partners)
    z_traces = [
        shifted(2, way, out_z.at[way], in_z.at[way], sa.at[4 + way], ra.at[4 + way]).start()
        for way in (0, 1)
    ]

    low = iota((FACE, 128), 1) < FACE
    swap = lambda a: pltpu.roll(a, FACE, 1)
    top, bottom = first[384:512, 384:512], first[0:128, 0:128]
    out_a[0] = jnp.where(low, swap(top[0:64]), top[64:128])
    out_a[1] = jnp.where(low, bottom[0:64], swap(bottom[64:128]))
    a_copies = [
        shifted(0, way, out_a.at[way], in_a.at[way], sa.at[way], ra.at[way]).start() for way in (0, 1)
    ]

    f_hi, f_lo = halves(first[...])
    tr[...] = dot1(f_hi, pick[...]) + dot1(f_lo, pick[...])
    ytop = [tr[128 * i + 96 : 128 * i + 128, 0:128] for i in range(4)]
    ybottom = [tr[128 * i : 128 * i + 32, 0:128] for i in range(4)]
    out_a[2] = jnp.where(low, jnp.concatenate(ytop[:2], 0), swap(jnp.concatenate(ytop[2:], 0)))
    out_a[3] = jnp.where(low, swap(jnp.concatenate(ybottom[:2], 0)), jnp.concatenate(ybottom[2:], 0))
    a_copies += [
        shifted(1, way, out_a.at[2 + way], in_a.at[2 + way], sa.at[2 + way], ra.at[2 + way]).start()
        for way in (0, 1)
    ]
    for copy in loads[4:]:
        copy.wait()

    v[...] = rhs[...] - dot3(u[...], mass[...])

    many = jnp.concatenate([restrict[...]] * 16, 0)
    lane_n = iota((N, 128), 1)
    first_half = lane_n < 64
    kind = (iota((384, 128), 1) % 64) // 8
    lift_r = jnp.where(kind == iota((384, 128), 0) // FACE + 1, dot3(lift[...], many, NT), 0.0)
    g = jnp.where(lane_n % 64 < 8, -dot3(mass[...], many, NT), 0.0)
    l_hi, l_lo = halves(lift_r[128:384])
    g = g + (dot1(pick[...], l_hi) + dot1(pick[...], l_lo))
    g = g + jnp.concatenate([lift_r[0:64], jnp.zeros((384, 128), F32), lift_r[64:128]], 0)
    g_hi, g_lo = halves(g)
    g_cat[...] = jnp.where(first_half, g_hi, g_lo)
    g_top[...] = jnp.where(first_half, g_hi, jnp.zeros_like(g_hi))
    rr = dot3(restrict[...], rhs[...], NT)
    lz[...] = dot3(lift[256:384, :], smoother[...])
    lz_hi, lz_lo = halves(lz[...])
    lzg[...] = dot1(lz_hi, g_cat[...]) + dot1(lz_lo, g_top[...])
    weight = 1.0 + jnp.sum(onehot[...], 0, keepdims=True)
    weight = jnp.broadcast_to(weight, (8, 128))
    per = 1.0 / weight
    d_row = 1.0 / jnp.concatenate([coef[s // 4, s % 4 : s % 4 + 1, :] for s in range(16)], 1)

    low32 = lane < FACE
    nothing = jnp.zeros((32, 128), F32)
    for s in range(16):
        x, y = s // 4, s % 4
        rows = slice(32 * s, 32 * s + 32)
        above = first[32 * s + 128 : 32 * s + 160, 0:128] if x < 3 else nothing
        below = first[32 * s - 128 : 32 * s - 96, 384:512] if x > 0 else nothing
        faces[rows, 0:128] = jnp.where(low32, above, below)
        above = tr[32 * s + 32 : 32 * s + 64, 0:128] if y < 3 else nothing
        below = tr[32 * s - 32 : 32 * s, 0:128] if y > 0 else nothing
        faces[rows, 128:256] = jnp.where(low32, below, above)
        own = tr[rows, 128:256]
        below = jnp.where(row == 0, 0.0, pltpu.roll(own, 1, 0))
        above = jnp.where(row == 31, 0.0, pltpu.roll(own, 31, 0))
        faces[rows, 256:384] = jnp.where(low32, below, above)

    for copy in a_copies:
        copy.wait_recv()
    faces[0:64, 0:128] = jnp.where(low, faces[0:64, 0:128], swap(in_a[0]))
    faces[64:128, 0:128] = jnp.where(low, faces[64:128, 0:128], in_a[0])
    faces[384:448, 0:128] = jnp.where(low, in_a[1], faces[384:448, 0:128])
    faces[448:512, 0:128] = jnp.where(low, swap(in_a[1]), faces[448:512, 0:128])
    for i in range(4):
        half = slice(32 * (i % 2), 32 * (i % 2) + 32)
        below, above = in_a[2, half, :], in_a[3, half, :]
        below = below if i < 2 else swap(below)
        above = swap(above) if i < 2 else above
        j = 128 * i
        faces[j : j + 32, 128:256] = jnp.where(low32, below, faces[j : j + 32, 128:256])
        j = 128 * i + 96
        faces[j : j + 32, 128:256] = jnp.where(low32, faces[j : j + 32, 128:256], above)

    v[...] = v[...] + dot3(faces[...], lift[...])
    u[...] = u[...] + dot3(v[...], smoother[...])
    s_hi, s_lo = halves(u[...])
    wide[...] = dot1(s_hi, g_cat[...]) + dot1(s_lo, g_top[...])

    for copy in z_traces:
        copy.wait_recv()
    low16 = iota((16, 128), 1) < FACE
    ends = jnp.concatenate([jnp.where(low16, in_z[0], 0.0), jnp.where(low16, 0.0, in_z[1])], 0)
    more = dot3(ends, lzg[...])
    wide[pl.ds(0, 16, stride=32), :] = wide[pl.ds(0, 16, stride=32), :] + more[0:16]
    wide[pl.ds(31, 16, stride=32), :] = wide[pl.ds(31, 16, stride=32), :] + more[16:32]
    w = wide[...].T
    w = w[0:64] + w[64:128]
    c[...] = jnp.concatenate([w[0:8] + rr, w[8:64] * d_row], 0)

    b_copies = [
        shifted(2, 0, c.at[40:48, :], in_bz.at[0], sb.at[4], rb.at[4]).start(),
        shifted(2, 1, c.at[48:56, :], in_bz.at[1], sb.at[5], rb.at[5]).start(),
        shifted(0, 0, c.at[16:24, 384:512], in_bx.at[0], sb.at[0], rb.at[0]).start(),
        shifted(0, 1, c.at[8:16, 0:128], in_bx.at[1], sb.at[1], rb.at[1]).start(),
        shifted(1, 0, c.at[24:32, :], in_by.at[0], sb.at[2], rb.at[2]).start(),
        shifted(1, 1, c.at[32:40, :], in_by.at[1], sb.at[3], rb.at[3]).start(),
    ]
    more = dot3(ends, lz[...])
    for start, part in ((0, more[0:16]), (31, more[16:32])):
        for s in range(16):
            at = 32 * s + start
            u[at : at + 1, :] = u[at : at + 1, :] + part[s : s + 1]
    first[...] = u[...] * d4(dcol[...])

    small = c[0:8, :]
    none8 = jnp.zeros((8, 128), F32)
    place = iota((8, N), 1)
    py, pz = (place // 32) % 4, place % 32
    small = small + jnp.concatenate([c[8:16, 128:512], none8], 1)
    small = small + jnp.concatenate([none8, c[16:24, 0:384]], 1)
    small = small + jnp.where(py > 0, pltpu.roll(c[24:32, :], 32, 1), 0.0)
    small = small + jnp.where(py < 3, pltpu.roll(c[32:40, :], N - 32, 1), 0.0)
    small = small + jnp.where(pz > 0, pltpu.roll(c[40:48, :], 1, 1), 0.0)
    small = small + jnp.where(pz < 31, pltpu.roll(c[48:56, :], N - 1, 1), 0.0)
    one = onehot[...].astype(BF16)
    r_hi, r_lo = halves(restrict[...])
    r_hi, r_lo = r_hi.astype(F32), r_lo.astype(F32)
    r_stack = jnp.concatenate([r_hi, r_hi, r_lo], 0).astype(BF16)

    for copy in b_copies:
        copy.wait_recv()
    zeros_mid = jnp.zeros((8, 256), F32)
    small = small + jnp.concatenate([in_bx[0], zeros_mid, in_bx[1]], 1)
    small = small + jnp.where(py == 0, pltpu.roll(in_by[0], N - 96, 1), 0.0)
    small = small + jnp.where(py == 3, pltpu.roll(in_by[1], 96, 1), 0.0)
    small = small + jnp.where(pz == 0, pltpu.roll(in_bz[0], N - 31, 1), 0.0)
    small = small + jnp.where(pz == 31, pltpu.roll(in_bz[1], 31, 1), 0.0)
    m_hi, m_lo = halves(small)
    parts = dot1(jnp.concatenate([m_hi.astype(F32), m_lo.astype(F32)], 0).astype(BF16), one)
    coarse_rhs = parts[0:8] + parts[8:16]
    zone = coarse_rhs * per
    zone_out[...] = zone

    z_copies = []
    for dim in (2, 1):
        for way in (0, 1):
            n = ngx - 1 + 2 * (dim - 1) + way
            z_copies.append(shifted(dim, way, zone_out, in_zone.at[n], sz.at[n], rz.at[n]).start())
    z_copies += [
        Message(zone_out, in_zone.at[n], sz.at[n], rz.at[n], device, None, None).start()
        for n, device in enumerate(line)
    ]

    two = zone + (coarse_rhs - (weight * dot3(cbm[...], zone) - zone)) * per

    for copy in z_copies:
        copy.wait_recv()
    total = in_zone[0]
    for n in range(1, ngx + 3):
        total = total + in_zone[n]
    two = two + total * per
    t_hi, t_lo = halves(two)
    t_hi, t_lo = t_hi.astype(F32), t_lo.astype(F32)
    t_stack = jnp.concatenate([t_hi, t_lo, t_hi], 0).astype(BF16)
    spread = lax.dot_general(t_stack, r_stack, TN, preferred_element_type=F32)
    e_hi, e_lo = halves(spread)
    spread = jnp.where(iota((128, N), 0) < 64, e_hi, e_lo)
    out_ref[...] = first[...] + dot1(one, spread)

    for copy in z_traces + a_copies + b_copies + z_copies:
        copy.wait_send()


def shards(sizes, rhs, coef, mass, smoother, lift, restrict, coarse_block_matrix, element_cluster_index):
    others = sizes[0] - 1 + 4
    hbm = pl.BlockSpec(memory_space=pl.ANY)
    dma = pltpu.SemaphoreType.DMA
    out = pl.pallas_call(
        functools.partial(kernel, sizes),
        out_shape=pltpu.VMEM((N, N), F32),
        in_specs=[hbm] * 8,
        out_specs=pl.BlockSpec(memory_space=pltpu.VMEM),
        scratch_shapes=[
            pltpu.VMEM((N, N), F32),
            pltpu.VMEM((N, N), F32),
            pltpu.VMEM((N, N), F32),
            pltpu.VMEM((384, N), F32),
            pltpu.VMEM((8, N), F32),
            pltpu.VMEM((8, 8), F32),
            pltpu.VMEM((4, 4, 32), F32),
            pltpu.VMEM((4, 4, 32), jnp.int32),
            pltpu.VMEM((N, 128), F32),
            pltpu.VMEM((N, 128), F32),
            pltpu.VMEM((N, 256), BF16),
            pltpu.VMEM((N, N), F32),
            pltpu.VMEM((N, N), F32),
            pltpu.VMEM((N, 256), F32),
            pltpu.VMEM((N, 384), F32),
            pltpu.VMEM((N, N), F32),
            pltpu.VMEM((N, 128), BF16),
            pltpu.VMEM((N, 128), BF16),
            pltpu.VMEM((128, N), F32),
            pltpu.VMEM((128, 128), F32),
            pltpu.VMEM((N, 128), F32),
            pltpu.VMEM((32, N), F32),
            pltpu.VMEM((4, FACE, 128), F32),
            pltpu.VMEM((4, FACE, 128), F32),
            pltpu.VMEM((2, 16, 128), F32),
            pltpu.VMEM((2, 16, 128), F32),
            pltpu.VMEM((FACE, N), F32),
            pltpu.VMEM((2, 8, 128), F32),
            pltpu.VMEM((2, 8, N), F32),
            pltpu.VMEM((2, 8, N), F32),
            pltpu.VMEM((8, 128), F32),
            pltpu.VMEM((others, 8, 128), F32),
            dma((10,)),
            dma((6,)),
            dma((6,)),
            dma((6,)),
            dma((6,)),
            dma((others,)),
            dma((others,)),
        ],
        compiler_params=pltpu.CompilerParams(
            collective_id=0, has_side_effects=True, vmem_limit_bytes=40 * 1024 * 1024
        ),
        name="cycle",
    )(*[
        pltpu.with_memory_space_constraint(a, pltpu.HBM)
        for a in (rhs.reshape(N, N), coef, mass, smoother, lift, restrict.T, coarse_block_matrix, element_cluster_index)
    ])
    return out.reshape(rhs.shape)


def solution(mesh):
    sizes = tuple(mesh.shape[a] for a in ("gx", "gy", "gz"))
    return jax.shard_map(
        functools.partial(shards, sizes),
        mesh=mesh,
        in_specs=(
            P("gx", "gy", "gz", None),
            P("gx", "gy", "gz"),
            P(),
            P(),
            P(),
            P(),
            P(),
            P("gx", "gy", "gz"),
        ),
        out_specs=P("gx", "gy", "gz", None),
        check_vma=False,
    )
```

```python
import functools

import jax
import jax.numpy as jnp
from jax import lax
from jax.experimental import pallas as pl
from jax.experimental.pallas import tpu as pltpu
from jax.sharding import PartitionSpec as P

N = 512
FACE = 64
F32 = jnp.float32
BF16 = jnp.bfloat16
MESH = pl.DeviceIdType.MESH
NT = (((1,), (1,)), ((), ()))
TN = (((0,), (0,)), ((), ()))
NN = (((1,), (0,)), ((), ()))


def dot3(a, b, dims=NN):
    return lax.dot_general(a, b, dims, precision=lax.Precision.HIGH, preferred_element_type=F32)


def halves(a):
    hi = a.astype(BF16)
    return hi, (a - hi.astype(F32)).astype(BF16)


def dot1(a, b):
    return jnp.dot(a, b, preferred_element_type=F32)


def iota(shape, dim):
    return lax.broadcasted_iota(jnp.int32, shape, dim)


def kernel(
    sizes, rhs_hbm, coef_hbm, mass_hbm, smoother_hbm, lift_hbm, restrict_hbm, cbm_hbm, label_hbm,
    out_ref,
    rhs, mass, smoother, lift, restrict, cbm, coef, label,
    dcol, onehot, pick, u, first, tr, faces, v, lsg, wide, rows_z,
    out_a, in_a, out_z, in_z, c, c_z, in_bx, in_by, in_bz, zone_out, in_zone,
    load_sem, sa, ra, sb, rb, sz, rz,
):
    ngx, ngy, ngz = sizes
    places = [lax.axis_index(axis) for axis in ("gx", "gy", "gz")]

    loads = [
        pltpu.make_async_copy(src, dst, load_sem.at[n])
        for n, (src, dst) in enumerate(
            [
                (coef_hbm, coef),
                (label_hbm, label),
                (rhs_hbm, rhs),
                (smoother_hbm, smoother),
                (restrict_hbm, restrict),
                (cbm_hbm, cbm),
                (mass_hbm, mass),
                (lift_hbm.at[FACE : 2 * FACE], lift.at[0:FACE]),
                (lift_hbm.at[0:FACE], lift.at[FACE : 2 * FACE]),
                (lift_hbm.at[2 * FACE :], lift.at[2 * FACE :]),
            ]
        )
    ]
    for copy in loads[:6]:
        copy.start()

    def along(dim, step):
        size = sizes[dim]
        return {("gx", "gy", "gz")[dim]: lax.rem(places[dim] + (step + size), size)}

    beside = [(along(dim, 1), along(dim, -1)) for dim in range(3)]
    there = [(places[dim] < sizes[dim] - 1, places[dim] > 0) for dim in range(3)]
    line = [along(0, step) for step in range(1, ngx)]

    barrier = pltpu.get_barrier_semaphore()
    for device in line:
        pl.semaphore_signal(barrier, inc=1, device_id=device, device_id_type=MESH)
    partners = ngx - 1
    for dim in (1, 2):
        for way in (0, 1):
            partners = partners + jnp.where(there[dim][way], 1, 0)

            @pl.when(there[dim][way])
            def _():
                pl.semaphore_signal(barrier, inc=1, device_id=beside[dim][way], device_id_type=MESH)

    class Message:
        def __init__(self, src, dst, send_sem, recv_sem, device, goes, comes):
            self.copy = pltpu.make_async_remote_copy(
                src_ref=src, dst_ref=dst, send_sem=send_sem, recv_sem=recv_sem,
                device_id=device, device_id_type=MESH,
            )
            self.goes, self.comes = goes, comes

        def start(self):
            self.when(self.goes, self.copy.start)
            return self

        def wait_recv(self):
            self.when(self.comes, self.copy.wait_recv)

        def wait_send(self):
            self.when(self.goes, self.copy.wait_send)

        def when(self, condition, act):
            if condition is None:
                act()
            else:
                pl.when(condition)(act)

    def shifted(dim, way, src, dst, send_sem, recv_sem):
        return Message(src, dst, send_sem, recv_sem, beside[dim][way], there[dim][way], there[dim][1 - way])

    for dim in range(3):
        for way in (0, 1):

            @pl.when(jnp.logical_not(there[dim][1 - way]))
            def _():
                if dim < 2:
                    in_a[2 * dim + way] = jnp.zeros((FACE, 128), F32)
                else:
                    in_z[way] = jnp.zeros((16, 128), F32)
                if dim == 0:
                    in_bx[way] = jnp.zeros((8, 128), F32)
                elif dim == 1:
                    in_by[way] = jnp.zeros((8, N), F32)
                else:
                    in_bz[way] = jnp.zeros((16, N), F32)
                if dim > 0:
                    in_zone[ngx - 1 + 2 * (dim - 1) + way] = jnp.zeros((8, 128), F32)

    node, face = iota((N, 256), 0), iota((N, 256), 1)
    block, within = face // FACE, face % FACE
    hi, lo = within // 8, within % 8
    end = jnp.where(block % 2 == 0, 7, 0)
    wanted = jnp.where(block < 2, hi * 64 + end * 8 + lo, hi * 64 + lo * 8 + end)
    pick[...] = jnp.where(node == wanted, 1.0, 0.0).astype(BF16)

    lane = iota((32, 128), 1)
    row = iota((32, 128), 0)

    def column(values):
        return jnp.sum(jnp.where(lane == row, jnp.broadcast_to(values, (32, 128)), 0.0), 1, keepdims=True)

    loads[0].wait()
    loads[1].wait()
    pad = jnp.zeros((1, 96), F32)
    for s in range(16):
        values = jnp.concatenate([coef[s // 4, s % 4 : s % 4 + 1, :], pad], 1)
        dcol[32 * s : 32 * s + 32, :] = jnp.broadcast_to(1.0 / column(values), (32, 128))
        names = jnp.concatenate([label[s // 4, s % 4 : s % 4 + 1, :].astype(F32), pad], 1)
        names = jnp.broadcast_to(column(names), (32, 128)).astype(jnp.int32)
        onehot[32 * s : 32 * s + 32, :] = jnp.where(names == lane % 64, 1.0, 0.0)
    d4 = lambda a: jnp.concatenate([a] * 4, 1)

    loads[2].wait()
    loads[3].wait()
    for copy in loads[6:]:
        copy.start()
    u[...] = dot3(rhs[...], smoother[...])
    first[...] = u[...] * d4(dcol[...])

    for s in range(16):
        rows_z[s : s + 1, :] = first[32 * s + 31 : 32 * s + 32, :]
        rows_z[16 + s : 17 + s, :] = first[32 * s : 32 * s + 1, :]
    ends = rows_z[...]
    e_hi, e_lo = halves(ends)
    ends = dot1(e_hi, pick[:, 128:256]) + dot1(e_lo, pick[:, 128:256])
    out_z[0] = ends[0:16]
    out_z[1] = ends[16:32]
    pl.semaphore_wait(barrier, partners)
    z_traces = [
        shifted(2, way, out_z.at[way], in_z.at[way], sa.at[4 + way], ra.at[4 + way]).start()
        for way in (0, 1)
    ]

    low = iota((FACE, 128), 1) < FACE
    swap = lambda a: pltpu.roll(a, FACE, 1)
    top, bottom = first[384:512, 384:512], first[0:128, 0:128]
    out_a[0] = jnp.where(low, swap(top[0:64]), top[64:128])
    out_a[1] = jnp.where(low, bottom[0:64], swap(bottom[64:128]))
    a_copies = [
        shifted(0, way, out_a.at[way], in_a.at[way], sa.at[way], ra.at[way]).start() for way in (0, 1)
    ]

    f_hi, f_lo = halves(first[...])
    tr[...] = dot1(f_hi, pick[...]) + dot1(f_lo, pick[...])
    ytop = [tr[128 * i + 96 : 128 * i + 128, 0:128] for i in range(4)]
    ybottom = [tr[128 * i : 128 * i + 32, 0:128] for i in range(4)]
    out_a[2] = jnp.where(low, jnp.concatenate(ytop[:2], 0), swap(jnp.concatenate(ytop[2:], 0)))
    out_a[3] = jnp.where(low, swap(jnp.concatenate(ybottom[:2], 0)), jnp.concatenate(ybottom[2:], 0))
    a_copies += [
        shifted(1, way, out_a.at[2 + way], in_a.at[2 + way], sa.at[2 + way], ra.at[2 + way]).start()
        for way in (0, 1)
    ]
    for copy in loads[4:]:
        copy.wait()

    lane_n = iota((N, 128), 1)
    first_half = lane_n < 64

    def table(a):
        hi, lo = halves(a)
        top = first_half[0 : a.shape[0]]
        return jnp.where(top, hi, lo), jnp.where(top, hi, jnp.zeros_like(hi))

    def project(a, columns):
        hi, lo = halves(a)
        t = dot1(hi, columns[0]) + dot1(lo, columns[1])
        return t + swap(t)

    many = jnp.concatenate([restrict[...]] * 16, 0)
    block = iota((384, 128), 0) // FACE
    kind = (iota((384, 128), 1) % 64) // 8
    lift_r = jnp.where(kind == jnp.where(block < 5, block + 1, 7), dot3(lift[...], many, NT), 0.0)
    g = jnp.where(lane_n % 64 < 8, -dot3(mass[...], many, NT), 0.0)
    l_hi, l_lo = halves(lift_r[128:384])
    g = g + (dot1(pick[...], l_hi) + dot1(pick[...], l_lo))
    g = g + jnp.concatenate([lift_r[0:64], jnp.zeros((384, 128), F32), lift_r[64:128]], 0)
    sg = project(smoother[...], table(g))
    sg_table = table(sg)
    lsg[...] = project(lift[...], sg_table)
    l_table = table(lsg[...])
    msg = project(mass[...], sg_table)
    own = jnp.where(lane_n % 64 < 8, many.T, 0.0)
    wide[...] = project(rhs[...], table(sg + own)) + project(u[...], table(g - msg))
    weight = 1.0 + jnp.sum(onehot[...], 0, keepdims=True)
    weight = jnp.broadcast_to(weight, (8, 128))
    per = 1.0 / weight
    d_row = 1.0 / jnp.concatenate([coef[s // 4, s % 4 : s % 4 + 1, :] for s in range(16)], 1)

    low32 = lane < FACE
    nothing = jnp.zeros((32, 128), F32)
    for s in range(16):
        x, y = s // 4, s % 4
        rows = slice(32 * s, 32 * s + 32)
        above = first[32 * s + 128 : 32 * s + 160, 0:128] if x < 3 else nothing
        below = first[32 * s - 128 : 32 * s - 96, 384:512] if x > 0 else nothing
        faces[rows, 0:128] = jnp.where(low32, above, below)
        above = tr[32 * s + 32 : 32 * s + 64, 0:128] if y < 3 else nothing
        below = tr[32 * s - 32 : 32 * s, 0:128] if y > 0 else nothing
        faces[rows, 128:256] = jnp.where(low32, below, above)
        own = tr[rows, 128:256]
        below = jnp.where(row == 0, 0.0, pltpu.roll(own, 1, 0))
        above = jnp.where(row == 31, 0.0, pltpu.roll(own, 31, 0))
        faces[rows, 256:384] = jnp.where(low32, below, above)

    for copy in a_copies:
        copy.wait_recv()
    faces[0:64, 0:128] = jnp.where(low, faces[0:64, 0:128], swap(in_a[0]))
    faces[64:128, 0:128] = jnp.where(low, faces[64:128, 0:128], in_a[0])
    faces[384:448, 0:128] = jnp.where(low, in_a[1], faces[384:448, 0:128])
    faces[448:512, 0:128] = jnp.where(low, swap(in_a[1]), faces[448:512, 0:128])
    for i in range(4):
        half = slice(32 * (i % 2), 32 * (i % 2) + 32)
        below, above = in_a[2, half, :], in_a[3, half, :]
        below = below if i < 2 else swap(below)
        above = swap(above) if i < 2 else above
        j = 128 * i
        faces[j : j + 32, 128:256] = jnp.where(low32, below, faces[j : j + 32, 128:256])
        j = 128 * i + 96
        faces[j : j + 32, 128:256] = jnp.where(low32, faces[j : j + 32, 128:256], above)

    wide[...] = wide[...] + project(faces[...], l_table)
    w = wide[...].T
    c_z[...] = jnp.concatenate([w[40:48] * d_row, jnp.broadcast_to(d_row, (8, N)), w[56:64] * d_row], 0)
    z_ways = [
        shifted(2, 0, c_z.at[0:16, :], in_bz.at[0], sb.at[4], rb.at[4]).start(),
        shifted(2, 1, c_z.at[8:24, :], in_bz.at[1], sb.at[5], rb.at[5]).start(),
    ]

    for copy in z_traces:
        copy.wait_recv()
    low16 = iota((16, 128), 1) < FACE
    ends = jnp.concatenate(
        [
            jnp.where(low16, in_z[0], 0.0),
            jnp.where(low16, 0.0, in_z[1]),
            jnp.where(low16, out_z[0], 0.0),
            jnp.where(low16, 0.0, out_z[1]),
        ],
        0,
    )
    more = dot3(ends, lsg[256:384, :])
    lane16 = iota((16, 128), 1)
    back = (lane16 >= 48) & (lane16 < 56)
    low_rows = more[0:16] + jnp.where(back, pltpu.roll(more[48:64], 8, 1), 0.0)
    high_rows = more[16:32] + jnp.where(back, pltpu.roll(more[32:48], 120, 1), 0.0)
    wide[pl.ds(0, 16, stride=32), :] = wide[pl.ds(0, 16, stride=32), :] + low_rows
    wide[pl.ds(31, 16, stride=32), :] = wide[pl.ds(31, 16, stride=32), :] + high_rows
    w = wide[...].T
    c[...] = jnp.concatenate([w[0:8], w[8:48] * d_row, w[48:56], w[56:64] * d_row], 0)

    b_copies = [
        shifted(0, 0, c.at[16:24, 384:512], in_bx.at[0], sb.at[0], rb.at[0]).start(),
        shifted(0, 1, c.at[8:16, 0:128], in_bx.at[1], sb.at[1], rb.at[1]).start(),
        shifted(1, 0, c.at[24:32, :], in_by.at[0], sb.at[2], rb.at[2]).start(),
        shifted(1, 1, c.at[32:40, :], in_by.at[1], sb.at[3], rb.at[3]).start(),
    ] + z_ways

    for s in range(16):
        at = 32 * s
        faces[at : at + 1, 256:384] = jnp.where(lane[0:1] < FACE, in_z[0, s : s + 1, :], faces[at : at + 1, 256:384])
        at = 32 * s + 31
        faces[at : at + 1, 256:384] = jnp.where(lane[0:1] < FACE, faces[at : at + 1, 256:384], in_z[1, s : s + 1, :])
    v[...] = rhs[...] - dot3(u[...], mass[...])

    small = c[0:8, :]
    none8 = jnp.zeros((8, 128), F32)
    place = iota((8, N), 1)
    py, pz = (place // 32) % 4, place % 32
    small = small + jnp.concatenate([c[8:16, 128:512], none8], 1)
    small = small + jnp.concatenate([none8, c[16:24, 0:384]], 1)
    small = small + jnp.where(py > 0, pltpu.roll(c[24:32, :], 32, 1), 0.0)
    small = small + jnp.where(py < 3, pltpu.roll(c[32:40, :], N - 32, 1), 0.0)
    small = small + jnp.where(pz > 0, pltpu.roll(c[40:48, :], 1, 1), 0.0)
    small = small + jnp.where(pz < 31, pltpu.roll(c[56:64, :], N - 1, 1), 0.0)
    one = onehot[...].astype(BF16)
    r_hi, r_lo = halves(restrict[...])
    r_hi, r_lo = r_hi.astype(F32), r_lo.astype(F32)
    r_stack = jnp.concatenate([r_hi, r_hi, r_lo], 0).astype(BF16)

    for copy in b_copies:
        copy.wait_recv()
    zeros_mid = jnp.zeros((8, 256), F32)
    small = small + jnp.concatenate([in_bx[0], zeros_mid, in_bx[1]], 1)
    small = small + jnp.where(py == 0, pltpu.roll(in_by[0], N - 96, 1), 0.0)
    small = small + jnp.where(py == 3, pltpu.roll(in_by[1], 96, 1), 0.0)
    z_low, z_high = pltpu.roll(in_bz[0], N - 31, 1), pltpu.roll(in_bz[1], 31, 1)
    small = small + jnp.where(pz == 0, z_low[0:8] + z_low[8:16] * c[48:56, :], 0.0)
    small = small + jnp.where(pz == 31, z_high[8:16] + z_high[0:8] * c[48:56, :], 0.0)
    m_hi, m_lo = halves(small)
    parts = dot1(jnp.concatenate([m_hi.astype(F32), m_lo.astype(F32)], 0).astype(BF16), one)
    coarse_rhs = parts[0:8] + parts[8:16]
    zone = coarse_rhs * per
    zone_out[...] = zone

    z_copies = []
    for dim in (2, 1):
        for way in (0, 1):
            n = ngx - 1 + 2 * (dim - 1) + way
            z_copies.append(shifted(dim, way, zone_out, in_zone.at[n], sz.at[n], rz.at[n]).start())
    z_copies += [
        Message(zone_out, in_zone.at[n], sz.at[n], rz.at[n], device, None, None).start()
        for n, device in enumerate(line)
    ]

    v[...] = v[...] + dot3(faces[...], lift[...])
    first[...] = (u[...] + dot3(v[...], smoother[...])) * d4(dcol[...])
    two = zone + (coarse_rhs - (weight * dot3(cbm[...], zone) - zone)) * per

    for copy in z_copies:
        copy.wait_recv()
    total = in_zone[0]
    for n in range(1, ngx + 3):
        total = total + in_zone[n]
    two = two + total * per
    t_hi, t_lo = halves(two)
    t_hi, t_lo = t_hi.astype(F32), t_lo.astype(F32)
    t_stack = jnp.concatenate([t_hi, t_lo, t_hi], 0).astype(BF16)
    spread = lax.dot_general(t_stack, r_stack, TN, preferred_element_type=F32)
    e_hi, e_lo = halves(spread)
    spread = jnp.where(iota((128, N), 0) < 64, e_hi, e_lo)
    out_ref[...] = first[...] + dot1(one, spread)

    for copy in z_traces + a_copies + b_copies + z_copies:
        copy.wait_send()


def shards(sizes, rhs, coef, mass, smoother, lift, restrict, coarse_block_matrix, element_cluster_index):
    others = sizes[0] - 1 + 4
    hbm = pl.BlockSpec(memory_space=pl.ANY)
    dma = pltpu.SemaphoreType.DMA
    out = pl.pallas_call(
        functools.partial(kernel, sizes),
        out_shape=pltpu.VMEM((N, N), F32),
        in_specs=[hbm] * 8,
        out_specs=pl.BlockSpec(memory_space=pltpu.VMEM),
        scratch_shapes=[
            pltpu.VMEM((N, N), F32),
            pltpu.VMEM((N, N), F32),
            pltpu.VMEM((N, N), F32),
            pltpu.VMEM((384, N), F32),
            pltpu.VMEM((8, N), F32),
            pltpu.VMEM((8, 8), F32),
            pltpu.VMEM((4, 4, 32), F32),
            pltpu.VMEM((4, 4, 32), jnp.int32),
            pltpu.VMEM((N, 128), F32),
            pltpu.VMEM((N, 128), F32),
            pltpu.VMEM((N, 256), BF16),
            pltpu.VMEM((N, N), F32),
            pltpu.VMEM((N, N), F32),
            pltpu.VMEM((N, 256), F32),
            pltpu.VMEM((N, 384), F32),
            pltpu.VMEM((N, N), F32),
            pltpu.VMEM((384, 128), F32),
            pltpu.VMEM((N, 128), F32),
            pltpu.VMEM((32, N), F32),
            pltpu.VMEM((4, FACE, 128), F32),
            pltpu.VMEM((4, FACE, 128), F32),
            pltpu.VMEM((2, 16, 128), F32),
            pltpu.VMEM((2, 16, 128), F32),
            pltpu.VMEM((FACE, N), F32),
            pltpu.VMEM((24, N), F32),
            pltpu.VMEM((2, 8, 128), F32),
            pltpu.VMEM((2, 8, N), F32),
            pltpu.VMEM((2, 16, N), F32),
            pltpu.VMEM((8, 128), F32),
            pltpu.VMEM((others, 8, 128), F32),
            dma((10,)),
            dma((6,)),
            dma((6,)),
            dma((6,)),
            dma((6,)),
            dma((others,)),
            dma((others,)),
        ],
        compiler_params=pltpu.CompilerParams(
            collective_id=0, has_side_effects=True, vmem_limit_bytes=40 * 1024 * 1024
        ),
        name="cycle",
    )(*[
        pltpu.with_memory_space_constraint(a, pltpu.HBM)
        for a in (rhs.reshape(N, N), coef, mass, smoother, lift, restrict.T, coarse_block_matrix, element_cluster_index)
    ])
    return out.reshape(rhs.shape)


def solution(mesh):
    sizes = tuple(mesh.shape[a] for a in ("gx", "gy", "gz"))
    return jax.shard_map(
        functools.partial(shards, sizes),
        mesh=mesh,
        in_specs=(
            P("gx", "gy", "gz", None),
            P("gx", "gy", "gz"),
            P(),
            P(),
            P(),
            P(),
            P(),
            P("gx", "gy", "gz"),
        ),
        out_specs=P("gx", "gy", "gz", None),
        check_vma=False,
    )
```

```python
import functools

import jax
import jax.numpy as jnp
from jax import lax
from jax.experimental import pallas as pl
from jax.experimental.pallas import tpu as pltpu
from jax.sharding import PartitionSpec as P

N = 512
FACE = 64
F32 = jnp.float32
BF16 = jnp.bfloat16
MESH = pl.DeviceIdType.MESH
NT = (((1,), (1,)), ((), ()))
TN = (((0,), (0,)), ((), ()))
NN = (((1,), (0,)), ((), ()))


def dot3(a, b, dims=NN):
    return lax.dot_general(a, b, dims, precision=lax.Precision.HIGH, preferred_element_type=F32)


def halves(a):
    hi = a.astype(BF16)
    return hi, (a - hi.astype(F32)).astype(BF16)


def dot1(a, b):
    return jnp.dot(a, b, preferred_element_type=F32)


def iota(shape, dim):
    return lax.broadcasted_iota(jnp.int32, shape, dim)


def kernel(
    sizes, rhs_hbm, coef_hbm, mass_hbm, smoother_hbm, lift_hbm, restrict_hbm, cbm_hbm, label_hbm,
    out_ref,
    rhs, mass, smoother, lift, restrict, cbm, coef, label,
    dcol, onehot, pick, u, first, tr, faces, v, lsg, wide, rows_z,
    out_a, in_a, out_z, in_z, c, out_by, out_bz, in_bx, in_by, in_bz, zone_out, in_zone,
    load_sem, sa, ra, sb, rb, sz, rz,
):
    ngx, ngy, ngz = sizes
    places = [lax.axis_index(axis) for axis in ("gx", "gy", "gz")]

    loads = [
        pltpu.make_async_copy(src, dst, load_sem.at[n])
        for n, (src, dst) in enumerate(
            [
                (coef_hbm, coef),
                (label_hbm, label),
                (rhs_hbm, rhs),
                (smoother_hbm, smoother),
                (restrict_hbm, restrict),
                (cbm_hbm, cbm),
                (mass_hbm, mass),
                (lift_hbm.at[FACE : 2 * FACE], lift.at[0:FACE]),
                (lift_hbm.at[0:FACE], lift.at[FACE : 2 * FACE]),
                (lift_hbm.at[2 * FACE :], lift.at[2 * FACE :]),
            ]
        )
    ]
    for copy in loads:
        copy.start()

    def along(dim, step):
        size = sizes[dim]
        return {("gx", "gy", "gz")[dim]: lax.rem(places[dim] + (step + size), size)}

    beside = [(along(dim, 1), along(dim, -1)) for dim in range(3)]
    there = [(places[dim] < sizes[dim] - 1, places[dim] > 0) for dim in range(3)]
    line = [along(0, step) for step in range(1, ngx)]

    barrier = pltpu.get_barrier_semaphore()
    for device in line:
        pl.semaphore_signal(barrier, inc=1, device_id=device, device_id_type=MESH)
    partners = ngx - 1
    for dim in (1, 2):
        for way in (0, 1):
            partners = partners + jnp.where(there[dim][way], 1, 0)

            @pl.when(there[dim][way])
            def _():
                pl.semaphore_signal(barrier, inc=1, device_id=beside[dim][way], device_id_type=MESH)

    class Message:
        def __init__(self, src, dst, send_sem, recv_sem, device, goes, comes):
            self.copy = pltpu.make_async_remote_copy(
                src_ref=src, dst_ref=dst, send_sem=send_sem, recv_sem=recv_sem,
                device_id=device, device_id_type=MESH,
            )
            self.goes, self.comes = goes, comes

        def start(self):
            self.when(self.goes, self.copy.start)
            return self

        def wait_recv(self):
            self.when(self.comes, self.copy.wait_recv)

        def wait_send(self):
            self.when(self.goes, self.copy.wait_send)

        def when(self, condition, act):
            if condition is None:
                act()
            else:
                pl.when(condition)(act)

    def shifted(dim, way, src, dst, send_sem, recv_sem):
        return Message(src, dst, send_sem, recv_sem, beside[dim][way], there[dim][way], there[dim][1 - way])

    for dim in range(3):
        for way in (0, 1):

            @pl.when(jnp.logical_not(there[dim][1 - way]))
            def _():
                if dim < 2:
                    in_a[2 * dim + way] = jnp.zeros((FACE, 128), F32)
                else:
                    in_z[way] = jnp.zeros((16, 128), F32)
                if dim == 0:
                    in_bx[way] = jnp.zeros((8, 128), F32)
                elif dim == 1:
                    in_by[way] = jnp.zeros((8, 128), F32)
                else:
                    in_bz[way] = jnp.zeros((16, 128), F32)
                if dim > 0:
                    in_zone[ngx - 1 + 2 * (dim - 1) + way] = jnp.zeros((8, 128), F32)

    node, face = iota((N, 256), 0), iota((N, 256), 1)
    block, within = face // FACE, face % FACE
    hi, lo = within // 8, within % 8
    end = jnp.where(block % 2 == 0, 7, 0)
    wanted = jnp.where(block < 2, hi * 64 + end * 8 + lo, hi * 64 + lo * 8 + end)
    pick[...] = jnp.where(node == wanted, 1.0, 0.0).astype(BF16)

    lane = iota((32, 128), 1)
    row = iota((32, 128), 0)

    def column(values):
        return jnp.sum(jnp.where(lane == row, jnp.broadcast_to(values, (32, 128)), 0.0), 1, keepdims=True)

    loads[0].wait()
    loads[1].wait()
    pad = jnp.zeros((1, 96), F32)
    for s in range(16):
        values = jnp.concatenate([coef[s // 4, s % 4 : s % 4 + 1, :], pad], 1)
        dcol[32 * s : 32 * s + 32, :] = jnp.broadcast_to(1.0 / column(values), (32, 128))
        names = jnp.concatenate([label[s // 4, s % 4 : s % 4 + 1, :].astype(F32), pad], 1)
        names = jnp.broadcast_to(column(names), (32, 128)).astype(jnp.int32)
        onehot[32 * s : 32 * s + 32, :] = jnp.where(names == lane % 64, 1.0, 0.0)
    d4 = lambda a: jnp.concatenate([a] * 4, 1)

    loads[2].wait()
    loads[3].wait()
    u[...] = dot3(rhs[...], smoother[...])
    first[...] = u[...] * d4(dcol[...])

    for s in range(16):
        rows_z[s : s + 1, :] = first[32 * s + 31 : 32 * s + 32, :]
        rows_z[16 + s : 17 + s, :] = first[32 * s : 32 * s + 1, :]
    ends = rows_z[...]
    e_hi, e_lo = halves(ends)
    ends = dot1(e_hi, pick[:, 128:256]) + dot1(e_lo, pick[:, 128:256])
    out_z[0] = ends[0:16]
    out_z[1] = ends[16:32]
    pl.semaphore_wait(barrier, partners)
    z_traces = [
        shifted(2, way, out_z.at[way], in_z.at[way], sa.at[4 + way], ra.at[4 + way]).start()
        for way in (0, 1)
    ]

    low = iota((FACE, 128), 1) < FACE
    swap = lambda a: pltpu.roll(a, FACE, 1)
    top, bottom = first[384:512, 384:512], first[0:128, 0:128]
    out_a[0] = jnp.where(low, swap(top[0:64]), top[64:128])
    out_a[1] = jnp.where(low, bottom[0:64], swap(bottom[64:128]))
    a_copies = [
        shifted(0, way, out_a.at[way], in_a.at[way], sa.at[way], ra.at[way]).start() for way in (0, 1)
    ]

    f_hi, f_lo = halves(first[...])
    tr[...] = dot1(f_hi, pick[...]) + dot1(f_lo, pick[...])
    ytop = [tr[128 * i + 96 : 128 * i + 128, 0:128] for i in range(4)]
    ybottom = [tr[128 * i : 128 * i + 32, 0:128] for i in range(4)]
    out_a[2] = jnp.where(low, jnp.concatenate(ytop[:2], 0), swap(jnp.concatenate(ytop[2:], 0)))
    out_a[3] = jnp.where(low, swap(jnp.concatenate(ybottom[:2], 0)), jnp.concatenate(ybottom[2:], 0))
    a_copies += [
        shifted(1, way, out_a.at[2 + way], in_a.at[2 + way], sa.at[2 + way], ra.at[2 + way]).start()
        for way in (0, 1)
    ]
    for copy in loads[4:]:
        copy.wait()

    lane_n = iota((N, 128), 1)
    first_half = lane_n < 64

    def table(a):
        hi, lo = halves(a)
        top = first_half[0 : a.shape[0]]
        return jnp.where(top, hi, lo), jnp.where(top, hi, jnp.zeros_like(hi))

    def project(a, columns):
        hi, lo = halves(a)
        t = dot1(hi, columns[0]) + dot1(lo, columns[1])
        return t + swap(t)

    many = jnp.concatenate([restrict[...]] * 16, 0)
    block = iota((384, 128), 0) // FACE
    kind = (iota((384, 128), 1) % 64) // 8
    r_wide = many.T
    r_table = table(r_wide)
    lift_r = jnp.where(kind == jnp.where(block < 5, block + 1, 7), project(lift[...], r_table), 0.0)
    g = jnp.where(lane_n % 64 < 8, -project(mass[...], r_table), 0.0)
    l_hi, l_lo = halves(lift_r[128:384])
    g = g + (dot1(pick[...], l_hi) + dot1(pick[...], l_lo))
    g = g + jnp.concatenate([lift_r[0:64], jnp.zeros((384, 128), F32), lift_r[64:128]], 0)
    sg = project(smoother[...], table(g))
    sg_table = table(sg)
    lsg[...] = project(lift[...], sg_table)
    l_table = table(lsg[...])
    msg = project(mass[...], sg_table)
    own = jnp.where(lane_n % 64 < 8, r_wide, 0.0)
    wide[...] = project(rhs[...], table(sg + own)) + project(u[...], table(g - msg))
    weight = 1.0 + jnp.sum(onehot[...], 0, keepdims=True)
    weight = jnp.broadcast_to(weight, (8, 128))
    per = 1.0 / weight
    d_row = 1.0 / jnp.concatenate([coef[s // 4, s % 4 : s % 4 + 1, :] for s in range(16)], 1)

    low32 = lane < FACE
    nothing = jnp.zeros((32, 128), F32)
    for s in range(16):
        x, y = s // 4, s % 4
        rows = slice(32 * s, 32 * s + 32)
        above = first[32 * s + 128 : 32 * s + 160, 0:128] if x < 3 else nothing
        below = first[32 * s - 128 : 32 * s - 96, 384:512] if x > 0 else nothing
        faces[rows, 0:128] = jnp.where(low32, above, below)
        above = tr[32 * s + 32 : 32 * s + 64, 0:128] if y < 3 else nothing
        below = tr[32 * s - 32 : 32 * s, 0:128] if y > 0 else nothing
        faces[rows, 128:256] = jnp.where(low32, below, above)
        own = tr[rows, 128:256]
        below = jnp.where(row == 0, 0.0, pltpu.roll(own, 1, 0))
        above = jnp.where(row == 31, 0.0, pltpu.roll(own, 31, 0))
        faces[rows, 256:384] = jnp.where(low32, below, above)

    for copy in a_copies:
        copy.wait_recv()
    faces[0:64, 0:128] = jnp.where(low, faces[0:64, 0:128], swap(in_a[0]))
    faces[64:128, 0:128] = jnp.where(low, faces[64:128, 0:128], in_a[0])
    faces[384:448, 0:128] = jnp.where(low, in_a[1], faces[384:448, 0:128])
    faces[448:512, 0:128] = jnp.where(low, swap(in_a[1]), faces[448:512, 0:128])
    for i in range(4):
        half = slice(32 * (i % 2), 32 * (i % 2) + 32)
        below, above = in_a[2, half, :], in_a[3, half, :]
        below = below if i < 2 else swap(below)
        above = swap(above) if i < 2 else above
        j = 128 * i
        faces[j : j + 32, 128:256] = jnp.where(low32, below, faces[j : j + 32, 128:256])
        j = 128 * i + 96
        faces[j : j + 32, 128:256] = jnp.where(low32, faces[j : j + 32, 128:256], above)

    wide[...] = wide[...] + project(faces[...], l_table)
    lane16 = iota((16, 128), 1)
    for way, at in ((0, 31), (1, 0)):
        d_ends = dcol[pl.ds(at, 16, stride=32), :]
        out_bz[way] = jnp.where(lane16 // 8 == 6, d_ends, d_ends * wide[pl.ds(at, 16, stride=32), :])
    z_ways = [
        shifted(2, way, out_bz.at[way], in_bz.at[way], sb.at[4 + way], rb.at[4 + way]).start() for way in (0, 1)
    ]

    for copy in z_traces:
        copy.wait_recv()
    low16 = iota((16, 128), 1) < FACE
    ends = jnp.concatenate(
        [
            jnp.where(low16, in_z[0], 0.0),
            jnp.where(low16, 0.0, in_z[1]),
            jnp.where(low16, out_z[0], 0.0),
            jnp.where(low16, 0.0, out_z[1]),
        ],
        0,
    )
    more = dot3(ends, lsg[256:384, :])
    wide[pl.ds(0, 16, stride=32), :] = wide[pl.ds(0, 16, stride=32), :] + more[0:16]
    wide[pl.ds(31, 16, stride=32), :] = wide[pl.ds(31, 16, stride=32), :] + more[16:32]
    w = wide[...].T
    c[...] = jnp.concatenate([w[0:8], w[8:64] * d_row], 0)
    quarter = iota((8, 128), 1) // 32

    def gather_y(tiles, turns):
        packed = jnp.zeros((8, 128), F32)
        for i in range(4):
            packed = jnp.where(quarter == i, pltpu.roll(tiles[i], turns[i], 1), packed)
        return packed

    out_by[0] = gather_y([c[24:32, 128 * i : 128 * i + 128] for i in range(4)], [32, 64, 96, 0])
    out_by[1] = gather_y([c[32:40, 128 * i : 128 * i + 128] for i in range(4)], [0, 32, 64, 96])

    b_copies = [
        shifted(0, 0, c.at[16:24, 384:512], in_bx.at[0], sb.at[0], rb.at[0]).start(),
        shifted(0, 1, c.at[8:16, 0:128], in_bx.at[1], sb.at[1], rb.at[1]).start(),
        shifted(1, 0, out_by.at[0], in_by.at[0], sb.at[2], rb.at[2]).start(),
        shifted(1, 1, out_by.at[1], in_by.at[1], sb.at[3], rb.at[3]).start(),
    ] + z_ways

    for s in range(16):
        at = 32 * s
        faces[at : at + 1, 256:384] = jnp.where(lane[0:1] < FACE, in_z[0, s : s + 1, :], faces[at : at + 1, 256:384])
        at = 32 * s + 31
        faces[at : at + 1, 256:384] = jnp.where(lane[0:1] < FACE, faces[at : at + 1, 256:384], in_z[1, s : s + 1, :])
    v[...] = rhs[...] - dot3(u[...], mass[...])

    small = c[0:8, :]
    none8 = jnp.zeros((8, 128), F32)
    place = iota((8, N), 1)
    py, pz = (place // 32) % 4, place % 32
    small = small + jnp.concatenate([c[8:16, 128:512], none8], 1)
    small = small + jnp.concatenate([none8, c[16:24, 0:384]], 1)
    small = small + jnp.where(py > 0, pltpu.roll(c[24:32, :], 32, 1), 0.0)
    small = small + jnp.where(py < 3, pltpu.roll(c[32:40, :], N - 32, 1), 0.0)
    small = small + jnp.where(pz > 0, pltpu.roll(c[40:48, :], 1, 1), 0.0)
    small = small + jnp.where(pz < 31, pltpu.roll(c[56:64, :], N - 1, 1), 0.0)
    one = onehot[...].astype(BF16)
    z_names = [onehot[pl.ds(0, 16, stride=32), :], onehot[pl.ds(31, 16, stride=32), :]]
    z_names = jnp.concatenate(z_names * 2, 0).astype(BF16)
    r_hi, r_lo = halves(restrict[...])
    r_hi, r_lo = r_hi.astype(F32), r_lo.astype(F32)
    r_stack = jnp.concatenate([r_hi, r_hi, r_lo], 0).astype(BF16)

    for copy in b_copies:
        copy.wait_recv()
    zeros_mid = jnp.zeros((8, 256), F32)
    small = small + jnp.concatenate([in_bx[0], zeros_mid, in_bx[1]], 1)
    below = [jnp.where(quarter == 0, pltpu.roll(in_by[0], turn, 1), 0.0) for turn in (0, 96, 64, 32)]
    above = [jnp.where(quarter == 3, pltpu.roll(in_by[1], turn, 1), 0.0) for turn in (96, 64, 32, 0)]
    small = small + jnp.concatenate([a + b for a, b in zip(below, above)], 1)
    z_low = in_bz[0] + pltpu.roll(in_bz[0], 120, 1) * more[48:64]
    z_high = in_bz[1] + pltpu.roll(in_bz[1], 8, 1) * more[32:48]
    z_add = jnp.concatenate([jnp.where(lane16 // 8 == 5, z_low, 0.0), jnp.where(lane16 // 8 == 7, z_high, 0.0)], 0)
    n_hi, n_lo = halves(z_add)
    z_add = jnp.concatenate([n_hi.astype(F32), n_lo.astype(F32)], 0).astype(BF16)
    z_add = lax.dot_general(z_add, z_names, TN, preferred_element_type=F32)
    m_hi, m_lo = halves(small)
    parts = dot1(jnp.concatenate([m_hi.astype(F32), m_lo.astype(F32)], 0).astype(BF16), one)
    coarse_rhs = parts[0:8] + parts[8:16] + (z_add[40:48] + z_add[56:64])
    zone = coarse_rhs * per
    zone_out[...] = zone

    z_copies = []
    for dim in (2, 1):
        for way in (0, 1):
            n = ngx - 1 + 2 * (dim - 1) + way
            z_copies.append(shifted(dim, way, zone_out, in_zone.at[n], sz.at[n], rz.at[n]).start())
    z_copies += [
        Message(zone_out, in_zone.at[n], sz.at[n], rz.at[n], device, None, None).start()
        for n, device in enumerate(line)
    ]

    v[...] = v[...] + dot3(faces[...], lift[...])
    first[...] = (u[...] + dot3(v[...], smoother[...])) * d4(dcol[...])
    two = zone + (coarse_rhs - (weight * dot3(cbm[...], zone) - zone)) * per

    for copy in z_copies:
        copy.wait_recv()
    total = in_zone[0]
    for n in range(1, ngx + 3):
        total = total + in_zone[n]
    two = two + total * per
    t_hi, t_lo = halves(two)
    t_hi, t_lo = t_hi.astype(F32), t_lo.astype(F32)
    t_stack = jnp.concatenate([t_hi, t_lo, t_hi], 0).astype(BF16)
    spread = lax.dot_general(t_stack, r_stack, TN, preferred_element_type=F32)
    e_hi, e_lo = halves(spread)
    spread = jnp.where(iota((128, N), 0) < 64, e_hi, e_lo)
    out_ref[...] = first[...] + dot1(one, spread)

    for copy in z_traces + a_copies + b_copies + z_copies:
        copy.wait_send()


def shards(sizes, rhs, coef, mass, smoother, lift, restrict, coarse_block_matrix, element_cluster_index):
    others = sizes[0] - 1 + 4
    hbm = pl.BlockSpec(memory_space=pl.ANY)
    dma = pltpu.SemaphoreType.DMA
    out = pl.pallas_call(
        functools.partial(kernel, sizes),
        out_shape=pltpu.VMEM((N, N), F32),
        in_specs=[hbm] * 8,
        out_specs=pl.BlockSpec(memory_space=pltpu.VMEM),
        scratch_shapes=[
            pltpu.VMEM((N, N), F32),
            pltpu.VMEM((N, N), F32),
            pltpu.VMEM((N, N), F32),
            pltpu.VMEM((384, N), F32),
            pltpu.VMEM((8, N), F32),
            pltpu.VMEM((8, 8), F32),
            pltpu.VMEM((4, 4, 32), F32),
            pltpu.VMEM((4, 4, 32), jnp.int32),
            pltpu.VMEM((N, 128), F32),
            pltpu.VMEM((N, 128), F32),
            pltpu.VMEM((N, 256), BF16),
            pltpu.VMEM((N, N), F32),
            pltpu.VMEM((N, N), F32),
            pltpu.VMEM((N, 256), F32),
            pltpu.VMEM((N, 384), F32),
            pltpu.VMEM((N, N), F32),
            pltpu.VMEM((384, 128), F32),
            pltpu.VMEM((N, 128), F32),
            pltpu.VMEM((32, N), F32),
            pltpu.VMEM((4, FACE, 128), F32),
            pltpu.VMEM((4, FACE, 128), F32),
            pltpu.VMEM((2, 16, 128), F32),
            pltpu.VMEM((2, 16, 128), F32),
            pltpu.VMEM((FACE, N), F32),
            pltpu.VMEM((2, 8, 128), F32),
            pltpu.VMEM((2, 16, 128), F32),
            pltpu.VMEM((2, 8, 128), F32),
            pltpu.VMEM((2, 8, 128), F32),
            pltpu.VMEM((2, 16, 128), F32),
            pltpu.VMEM((8, 128), F32),
            pltpu.VMEM((others, 8, 128), F32),
            dma((10,)),
            dma((6,)),
            dma((6,)),
            dma((6,)),
            dma((6,)),
            dma((others,)),
            dma((others,)),
        ],
        compiler_params=pltpu.CompilerParams(
            collective_id=0, has_side_effects=True, vmem_limit_bytes=40 * 1024 * 1024
        ),
        name="cycle",
    )(*[
        pltpu.with_memory_space_constraint(a, pltpu.HBM)
        for a in (rhs.reshape(N, N), coef, mass, smoother, lift, restrict.T, coarse_block_matrix, element_cluster_index)
    ])
    return out.reshape(rhs.shape)


def solution(mesh):
    sizes = tuple(mesh.shape[a] for a in ("gx", "gy", "gz"))
    return jax.shard_map(
        functools.partial(shards, sizes),
        mesh=mesh,
        in_specs=(
            P("gx", "gy", "gz", None),
            P("gx", "gy", "gz"),
            P(),
            P(),
            P(),
            P(),
            P(),
            P("gx", "gy", "gz"),
        ),
        out_specs=P("gx", "gy", "gz", None),
        check_vma=False,
    )
```

```python
import functools

import jax
import jax.numpy as jnp
from jax import lax
from jax.experimental import pallas as pl
from jax.experimental.pallas import tpu as pltpu
from jax.sharding import PartitionSpec as P

N = 512
FACE = 64
F32 = jnp.float32
BF16 = jnp.bfloat16
MESH = pl.DeviceIdType.MESH
NT = (((1,), (1,)), ((), ()))
TN = (((0,), (0,)), ((), ()))
NN = (((1,), (0,)), ((), ()))


def dot3(a, b, dims=NN):
    return lax.dot_general(a, b, dims, precision=lax.Precision.HIGH, preferred_element_type=F32)


def halves(a):
    hi = a.astype(BF16)
    return hi, (a - hi.astype(F32)).astype(BF16)


def dot1(a, b):
    return jnp.dot(a, b, preferred_element_type=F32)


def iota(shape, dim):
    return lax.broadcasted_iota(jnp.int32, shape, dim)


def kernel(
    sizes, rhs_hbm, coef_hbm, mass_hbm, smoother_hbm, lift_hbm, restrict_hbm, cbm_hbm, label_hbm,
    out_ref,
    rhs, mass, smoother, lift, restrict, cbm, coef, label,
    dcol, onehot, pick, u, first, tr, faces, v, lsg, wide, scatter, s_off, m_hi, m_lo,
    out_a, in_a, out_z, in_z, c, out_by, out_bz, in_bx, in_by, in_bz, zone_out, in_zone,
    load_sem, sa, ra, sb, rb, sz, rz,
):
    ngx, ngy, ngz = sizes
    places = [lax.axis_index(axis) for axis in ("gx", "gy", "gz")]

    def along(dim, step):
        size = sizes[dim]
        return {("gx", "gy", "gz")[dim]: lax.rem(places[dim] + (step + size), size)}

    beside = [(along(dim, 1), along(dim, -1)) for dim in range(3)]
    there = [(places[dim] < sizes[dim] - 1, places[dim] > 0) for dim in range(3)]
    line = [along(0, step) for step in range(1, ngx)]

    barrier = pltpu.get_barrier_semaphore()
    partners = ngx - 1
    for dim in (2, 1):
        for way in (0, 1):
            partners = partners + jnp.where(there[dim][way], 1, 0)

            @pl.when(there[dim][way])
            def _():
                pl.semaphore_signal(barrier, inc=1, device_id=beside[dim][way], device_id_type=MESH)
    for device in line:
        pl.semaphore_signal(barrier, inc=1, device_id=device, device_id_type=MESH)

    loads = [
        pltpu.make_async_copy(src, dst, load_sem.at[n])
        for n, (src, dst) in enumerate(
            [
                (coef_hbm, coef),
                (label_hbm, label),
                (rhs_hbm, rhs),
                (smoother_hbm, smoother),
                (restrict_hbm, restrict),
                (cbm_hbm, cbm),
                (mass_hbm, mass),
                (lift_hbm.at[FACE : 2 * FACE], lift.at[0:FACE]),
                (lift_hbm.at[0:FACE], lift.at[FACE : 2 * FACE]),
                (lift_hbm.at[2 * FACE :], lift.at[2 * FACE :]),
            ]
        )
    ]
    for copy in loads:
        copy.start()

    class Message:
        def __init__(self, src, dst, send_sem, recv_sem, device, goes, comes):
            self.copy = pltpu.make_async_remote_copy(
                src_ref=src, dst_ref=dst, send_sem=send_sem, recv_sem=recv_sem,
                device_id=device, device_id_type=MESH,
            )
            self.goes, self.comes = goes, comes

        def start(self):
            self.when(self.goes, self.copy.start)
            return self

        def wait_recv(self):
            self.when(self.comes, self.copy.wait_recv)

        def wait_send(self):
            self.when(self.goes, self.copy.wait_send)

        def when(self, condition, act):
            if condition is None:
                act()
            else:
                pl.when(condition)(act)

    def shifted(dim, way, src, dst, send_sem, recv_sem):
        return Message(src, dst, send_sem, recv_sem, beside[dim][way], there[dim][way], there[dim][1 - way])

    for dim in range(3):
        for way in (0, 1):

            @pl.when(jnp.logical_not(there[dim][1 - way]))
            def _():
                if dim < 2:
                    in_a[2 * dim + way] = jnp.zeros((FACE, 128), F32)
                else:
                    in_z[way] = jnp.zeros((16, 128), F32)
                if dim == 0:
                    in_bx[way] = jnp.zeros((8, 128), F32)
                elif dim == 1:
                    in_by[way] = jnp.zeros((8, 128), F32)
                else:
                    in_bz[way] = jnp.zeros((16, 128), F32)
                if dim > 0:
                    in_zone[ngx - 1 + 2 * (dim - 1) + way] = jnp.zeros((8, 128), F32)

    node, face = iota((N, 256), 0), iota((N, 256), 1)
    block, within = face // FACE, face % FACE
    hi, lo = within // 8, within % 8
    end = jnp.where(block % 2 == 0, 7, 0)
    wanted = jnp.where(block < 2, hi * 64 + end * 8 + lo, hi * 64 + lo * 8 + end)
    pick[...] = jnp.where(node == wanted, 1.0, 0.0).astype(BF16)

    lane = iota((32, 128), 1)
    row = iota((32, 128), 0)

    def column(values):
        return jnp.sum(jnp.where(lane == row, jnp.broadcast_to(values, (32, 128)), 0.0), 1, keepdims=True)

    loads[0].wait()
    loads[1].wait()
    pad = jnp.zeros((1, 96), F32)
    for s in range(16):
        values = jnp.concatenate([coef[s // 4, s % 4 : s % 4 + 1, :], pad], 1)
        dcol[32 * s : 32 * s + 32, :] = jnp.broadcast_to(1.0 / column(values), (32, 128))
        names = jnp.concatenate([label[s // 4, s % 4 : s % 4 + 1, :].astype(F32), pad], 1)
        names = jnp.broadcast_to(column(names), (32, 128)).astype(jnp.int32)
        onehot[32 * s : 32 * s + 32, :] = jnp.where(names == lane % 64, 1.0, 0.0)
    d4 = lambda a: jnp.concatenate([a] * 4, 1)

    loads[2].wait()
    loads[3].wait()
    u[...] = dot3(rhs[...], smoother[...])
    first[...] = u[...] * d4(dcol[...])

    low = iota((FACE, 128), 1) < FACE
    swap = lambda a: pltpu.roll(a, FACE, 1)
    top, bottom = first[384:512, 384:512], first[0:128, 0:128]
    out_a[0] = jnp.where(low, swap(top[0:64]), top[64:128])
    out_a[1] = jnp.where(low, bottom[0:64], swap(bottom[64:128]))
    f_hi, f_lo = halves(first[...])
    tr[...] = dot1(f_hi, pick[...]) + dot1(f_lo, pick[...])
    ytop = [tr[128 * i + 96 : 128 * i + 128, 0:128] for i in range(4)]
    ybottom = [tr[128 * i : 128 * i + 32, 0:128] for i in range(4)]
    out_a[2] = jnp.where(low, jnp.concatenate(ytop[:2], 0), swap(jnp.concatenate(ytop[2:], 0)))
    out_a[3] = jnp.where(low, swap(jnp.concatenate(ybottom[:2], 0)), jnp.concatenate(ybottom[2:], 0))
    for i in range(16):
        out_z[0, i : i + 1, :] = tr[32 * i + 31 : 32 * i + 32, 128:256]
        out_z[1, i : i + 1, :] = tr[32 * i : 32 * i + 1, 128:256]
    pl.semaphore_wait(barrier, partners)
    z_traces = [
        shifted(2, way, out_z.at[way], in_z.at[way], sa.at[4 + way], ra.at[4 + way]).start()
        for way in (0, 1)
    ]
    a_copies = [
        shifted(dim, way, out_a.at[2 * dim + way], in_a.at[2 * dim + way], sa.at[2 * dim + way], ra.at[2 * dim + way]).start()
        for dim in (1, 0)
        for way in (0, 1)
    ]

    for copy in loads[4:]:
        copy.wait()

    lane_n = iota((N, 128), 1)
    first_half = lane_n < 64

    def table(a):
        hi, lo = halves(a)
        top = first_half[0 : a.shape[0]]
        return jnp.where(top, hi, lo), jnp.where(top, hi, jnp.zeros_like(hi))

    def project(a, columns):
        hi, lo = halves(a)
        t = dot1(hi, columns[0]) + dot1(lo, columns[1])
        return t + swap(t)

    many = jnp.concatenate([restrict[...]] * 16, 0)
    block = iota((384, 128), 0) // FACE
    kind = (iota((384, 128), 1) % 64) // 8
    r_wide = many.T
    r_table = table(r_wide)
    lift_r = jnp.where(kind == jnp.where(block < 5, block + 1, 7), project(lift[...], r_table), 0.0)
    unit = jnp.where(iota((128, 128), 0) == iota((128, 128), 1), 1.0, 0.0)
    m_hi[...], m_lo[...] = halves(mass[...])
    for i in range(4):
        part = slice(128 * i, 128 * i + 128)
        m_hi[part, part], m_lo[part, part] = halves(mass[part, part] - unit)

    def mass_rest(columns):
        t = dot1(m_hi[...], columns[0]) + dot1(m_lo[...], columns[1])
        return t + swap(t)

    scatter[...] = jnp.where(lane_n % 64 < 8, -(r_wide + mass_rest(r_table)), 0.0)
    scatter[0:64, :] = scatter[0:64, :] + lift_r[0:64]
    scatter[448:512, :] = scatter[448:512, :] + lift_r[64:128]
    for i in range(8):
        for j, at in ((7, 128), (0, 192)):
            rows = slice(64 * i + 8 * j, 64 * i + 8 * j + 8)
            scatter[rows, :] = scatter[rows, :] + lift_r[at + 8 * i : at + 8 * i + 8]
    for k, at in ((7, 256), (0, 320)):
        rows = pl.ds(k, FACE, stride=8)
        scatter[rows, :] = scatter[rows, :] + lift_r[at : at + FACE]
    g = scatter[...]

    s_off[...] = smoother[...].astype(BF16)
    for i in range(4):
        part = slice(128 * i, 128 * i + 128)
        s_off[part, part] = (smoother[part, part] - unit).astype(BF16)
    t = dot1(s_off[...], table(g)[0])
    s_rest = t + swap(t)
    sg = g + s_rest
    sg_table = table(sg)
    lsg[...] = project(lift[...], sg_table)
    l_table = table(lsg[...])
    small_g = -(s_rest + mass_rest(sg_table))
    own = jnp.where(lane_n % 64 < 8, r_wide, 0.0)
    t = dot1(u[...].astype(BF16), table(small_g)[0])
    wide[...] = project(rhs[...], table(sg + own)) + (t + swap(t))
    weight = 1.0 + jnp.sum(onehot[...], 0, keepdims=True)
    weight = jnp.broadcast_to(weight, (8, 128))
    per = 1.0 / weight
    d_row = 1.0 / jnp.concatenate([coef[s // 4, s % 4 : s % 4 + 1, :] for s in range(16)], 1)

    low32 = lane < FACE
    nothing = jnp.zeros((32, 128), F32)
    for s in range(16):
        x, y = s // 4, s % 4
        rows = slice(32 * s, 32 * s + 32)
        above = first[32 * s + 128 : 32 * s + 160, 0:128] if x < 3 else nothing
        below = first[32 * s - 128 : 32 * s - 96, 384:512] if x > 0 else nothing
        faces[rows, 0:128] = jnp.where(low32, above, below)
        above = tr[32 * s + 32 : 32 * s + 64, 0:128] if y < 3 else nothing
        below = tr[32 * s - 32 : 32 * s, 0:128] if y > 0 else nothing
        faces[rows, 128:256] = jnp.where(low32, below, above)
        own = tr[rows, 128:256]
        below = jnp.where(row == 0, 0.0, pltpu.roll(own, 1, 0))
        above = jnp.where(row == 31, 0.0, pltpu.roll(own, 31, 0))
        faces[rows, 256:384] = jnp.where(low32, below, above)

    for copy in a_copies:
        copy.wait_recv()
    faces[0:64, 0:128] = jnp.where(low, faces[0:64, 0:128], swap(in_a[0]))
    faces[64:128, 0:128] = jnp.where(low, faces[64:128, 0:128], in_a[0])
    faces[384:448, 0:128] = jnp.where(low, in_a[1], faces[384:448, 0:128])
    faces[448:512, 0:128] = jnp.where(low, swap(in_a[1]), faces[448:512, 0:128])
    for i in range(4):
        half = slice(32 * (i % 2), 32 * (i % 2) + 32)
        below, above = in_a[2, half, :], in_a[3, half, :]
        below = below if i < 2 else swap(below)
        above = swap(above) if i < 2 else above
        j = 128 * i
        faces[j : j + 32, 128:256] = jnp.where(low32, below, faces[j : j + 32, 128:256])
        j = 128 * i + 96
        faces[j : j + 32, 128:256] = jnp.where(low32, faces[j : j + 32, 128:256], above)

    wide[...] = wide[...] + project(faces[...], l_table)
    lane16 = iota((16, 128), 1)
    for way, at in ((0, 31), (1, 0)):
        d_ends = dcol[pl.ds(at, 16, stride=32), :]
        out_bz[way] = jnp.where(lane16 // 8 == 6, d_ends, d_ends * wide[pl.ds(at, 16, stride=32), :])
    z_ways = [
        shifted(2, way, out_bz.at[way], in_bz.at[way], sb.at[4 + way], rb.at[4 + way]).start() for way in (0, 1)
    ]

    for copy in z_traces:
        copy.wait_recv()
    low16 = iota((16, 128), 1) < FACE
    ends = jnp.concatenate(
        [
            jnp.where(low16, in_z[0], 0.0),
            jnp.where(low16, 0.0, in_z[1]),
            jnp.where(low16, out_z[0], 0.0),
            jnp.where(low16, 0.0, out_z[1]),
        ],
        0,
    )
    more = dot3(ends, lsg[256:384, :])
    wide[pl.ds(0, 16, stride=32), :] = wide[pl.ds(0, 16, stride=32), :] + more[0:16]
    wide[pl.ds(31, 16, stride=32), :] = wide[pl.ds(31, 16, stride=32), :] + more[16:32]
    w = wide[...].T
    c[...] = jnp.concatenate([w[0:8], w[8:64] * d_row], 0)
    quarter = iota((8, 128), 1) // 32

    def gather_y(tiles, turns):
        packed = jnp.zeros((8, 128), F32)
        for i in range(4):
            packed = jnp.where(quarter == i, pltpu.roll(tiles[i], turns[i], 1), packed)
        return packed

    out_by[0] = gather_y([c[24:32, 128 * i : 128 * i + 128] for i in range(4)], [32, 64, 96, 0])
    out_by[1] = gather_y([c[32:40, 128 * i : 128 * i + 128] for i in range(4)], [0, 32, 64, 96])

    b_copies = [
        shifted(0, 0, c.at[16:24, 384:512], in_bx.at[0], sb.at[0], rb.at[0]).start(),
        shifted(0, 1, c.at[8:16, 0:128], in_bx.at[1], sb.at[1], rb.at[1]).start(),
        shifted(1, 0, out_by.at[0], in_by.at[0], sb.at[2], rb.at[2]).start(),
        shifted(1, 1, out_by.at[1], in_by.at[1], sb.at[3], rb.at[3]).start(),
    ] + z_ways

    for s in range(16):
        at = 32 * s
        faces[at : at + 1, 256:384] = jnp.where(lane[0:1] < FACE, in_z[0, s : s + 1, :], faces[at : at + 1, 256:384])
        at = 32 * s + 31
        faces[at : at + 1, 256:384] = jnp.where(lane[0:1] < FACE, faces[at : at + 1, 256:384], in_z[1, s : s + 1, :])
    u_hi, u_lo = halves(u[...])
    v[...] = rhs[...] - (u[...] + (dot1(u_hi, m_hi[...]) + dot1(u_lo, m_hi[...]) + dot1(u_hi, m_lo[...])))

    small = c[0:8, :]
    none8 = jnp.zeros((8, 128), F32)
    place = iota((8, N), 1)
    py, pz = (place // 32) % 4, place % 32
    small = small + jnp.concatenate([c[8:16, 128:512], none8], 1)
    small = small + jnp.concatenate([none8, c[16:24, 0:384]], 1)
    small = small + jnp.where(py > 0, pltpu.roll(c[24:32, :], 32, 1), 0.0)
    small = small + jnp.where(py < 3, pltpu.roll(c[32:40, :], N - 32, 1), 0.0)
    small = small + jnp.where(pz > 0, pltpu.roll(c[40:48, :], 1, 1), 0.0)
    small = small + jnp.where(pz < 31, pltpu.roll(c[56:64, :], N - 1, 1), 0.0)
    one = onehot[...].astype(BF16)
    z_names = [onehot[pl.ds(0, 16, stride=32), :], onehot[pl.ds(31, 16, stride=32), :]]
    z_names = jnp.concatenate(z_names * 2, 0).astype(BF16)
    r_hi, r_lo = halves(restrict[...])
    r_hi, r_lo = r_hi.astype(F32), r_lo.astype(F32)
    r_stack = jnp.concatenate([r_hi, r_hi, r_lo], 0).astype(BF16)

    for copy in b_copies:
        copy.wait_recv()
    zeros_mid = jnp.zeros((8, 256), F32)
    small = small + jnp.concatenate([in_bx[0], zeros_mid, in_bx[1]], 1)
    below = [jnp.where(quarter == 0, pltpu.roll(in_by[0], turn, 1), 0.0) for turn in (0, 96, 64, 32)]
    above = [jnp.where(quarter == 3, pltpu.roll(in_by[1], turn, 1), 0.0) for turn in (96, 64, 32, 0)]
    small = small + jnp.concatenate([a + b for a, b in zip(below, above)], 1)
    z_low = in_bz[0] + pltpu.roll(in_bz[0], 120, 1) * more[48:64]
    z_high = in_bz[1] + pltpu.roll(in_bz[1], 8, 1) * more[32:48]
    z_add = jnp.concatenate([jnp.where(lane16 // 8 == 5, z_low, 0.0), jnp.where(lane16 // 8 == 7, z_high, 0.0)], 0)
    n_hi, n_lo = halves(z_add)
    z_add = jnp.concatenate([n_hi.astype(F32), n_lo.astype(F32)], 0).astype(BF16)
    z_add = lax.dot_general(z_add, z_names, TN, preferred_element_type=F32)
    q_hi, q_lo = halves(small)
    parts = dot1(jnp.concatenate([q_hi.astype(F32), q_lo.astype(F32)], 0).astype(BF16), one)
    coarse_rhs = parts[0:8] + parts[8:16] + (z_add[40:48] + z_add[56:64])
    zone = coarse_rhs * per
    zone_out[...] = zone

    z_copies = []
    for dim in (2, 1):
        for way in (0, 1):
            n = ngx - 1 + 2 * (dim - 1) + way
            z_copies.append(shifted(dim, way, zone_out, in_zone.at[n], sz.at[n], rz.at[n]).start())
    z_copies += [
        Message(zone_out, in_zone.at[n], sz.at[n], rz.at[n], device, None, None).start()
        for n, device in enumerate(line)
    ]

    v[...] = v[...] + dot3(faces[...], lift[...])
    first[...] = (u[...] + dot3(v[...], smoother[...])) * d4(dcol[...])
    two = zone + (coarse_rhs - (weight * dot3(cbm[...], zone) - zone)) * per

    for copy in z_copies:
        copy.wait_recv()
    total = in_zone[0]
    for n in range(1, ngx + 3):
        total = total + in_zone[n]
    two = two + total * per
    t_hi, t_lo = halves(two)
    t_hi, t_lo = t_hi.astype(F32), t_lo.astype(F32)
    t_stack = jnp.concatenate([t_hi, t_lo, t_hi], 0).astype(BF16)
    spread = lax.dot_general(t_stack, r_stack, TN, preferred_element_type=F32)
    e_hi, e_lo = halves(spread)
    spread = jnp.where(iota((128, N), 0) < 64, e_hi, e_lo)
    out_ref[...] = first[...] + dot1(one, spread)

    for copy in z_traces + a_copies + b_copies + z_copies:
        copy.wait_send()


def shards(sizes, rhs, coef, mass, smoother, lift, restrict, coarse_block_matrix, element_cluster_index):
    others = sizes[0] - 1 + 4
    hbm = pl.BlockSpec(memory_space=pl.ANY)
    dma = pltpu.SemaphoreType.DMA
    out = pl.pallas_call(
        functools.partial(kernel, sizes),
        out_shape=pltpu.VMEM((N, N), F32),
        in_specs=[hbm] * 8,
        out_specs=pl.BlockSpec(memory_space=pltpu.VMEM),
        scratch_shapes=[
            pltpu.VMEM((N, N), F32),
            pltpu.VMEM((N, N), F32),
            pltpu.VMEM((N, N), F32),
            pltpu.VMEM((384, N), F32),
            pltpu.VMEM((8, N), F32),
            pltpu.VMEM((8, 8), F32),
            pltpu.VMEM((4, 4, 32), F32),
            pltpu.VMEM((4, 4, 32), jnp.int32),
            pltpu.VMEM((N, 128), F32),
            pltpu.VMEM((N, 128), F32),
            pltpu.VMEM((N, 256), BF16),
            pltpu.VMEM((N, N), F32),
            pltpu.VMEM((N, N), F32),
            pltpu.VMEM((N, 256), F32),
            pltpu.VMEM((N, 384), F32),
            pltpu.VMEM((N, N), F32),
            pltpu.VMEM((384, 128), F32),
            pltpu.VMEM((N, 128), F32),
            pltpu.VMEM((N, 128), F32),
            pltpu.VMEM((N, N), BF16),
            pltpu.VMEM((N, N), BF16),
            pltpu.VMEM((N, N), BF16),
            pltpu.VMEM((4, FACE, 128), F32),
            pltpu.VMEM((4, FACE, 128), F32),
            pltpu.VMEM((2, 16, 128), F32),
            pltpu.VMEM((2, 16, 128), F32),
            pltpu.VMEM((FACE, N), F32),
            pltpu.VMEM((2, 8, 128), F32),
            pltpu.VMEM((2, 16, 128), F32),
            pltpu.VMEM((2, 8, 128), F32),
            pltpu.VMEM((2, 8, 128), F32),
            pltpu.VMEM((2, 16, 128), F32),
            pltpu.VMEM((8, 128), F32),
            pltpu.VMEM((others, 8, 128), F32),
            dma((10,)),
            dma((6,)),
            dma((6,)),
            dma((6,)),
            dma((6,)),
            dma((others,)),
            dma((others,)),
        ],
        compiler_params=pltpu.CompilerParams(
            collective_id=0, has_side_effects=True, vmem_limit_bytes=40 * 1024 * 1024
        ),
        name="cycle",
    )(*[
        pltpu.with_memory_space_constraint(a, pltpu.HBM)
        for a in (rhs.reshape(N, N), coef, mass, smoother, lift, restrict.T, coarse_block_matrix, element_cluster_index)
    ])
    return out.reshape(rhs.shape)


def solution(mesh):
    sizes = tuple(mesh.shape[a] for a in ("gx", "gy", "gz"))
    return jax.shard_map(
        functools.partial(shards, sizes),
        mesh=mesh,
        in_specs=(
            P("gx", "gy", "gz", None),
            P("gx", "gy", "gz"),
            P(),
            P(),
            P(),
            P(),
            P(),
            P("gx", "gy", "gz"),
        ),
        out_specs=P("gx", "gy", "gz", None),
        check_vma=False,
    )
```

```python
import functools

import jax
import jax.numpy as jnp
from jax import lax
from jax.experimental import pallas as pl
from jax.experimental.pallas import tpu as pltpu
from jax.sharding import PartitionSpec as P

N = 512
FACE = 64
F32 = jnp.float32
BF16 = jnp.bfloat16
MESH = pl.DeviceIdType.MESH
NT = (((1,), (1,)), ((), ()))
TN = (((0,), (0,)), ((), ()))
NN = (((1,), (0,)), ((), ()))


def dot3(a, b, dims=NN):
    return lax.dot_general(a, b, dims, precision=lax.Precision.HIGH, preferred_element_type=F32)


def halves(a):
    hi = a.astype(BF16)
    return hi, (a - hi.astype(F32)).astype(BF16)


def dot1(a, b):
    return jnp.dot(a, b, preferred_element_type=F32)


def iota(shape, dim):
    return lax.broadcasted_iota(jnp.int32, shape, dim)


def kernel(
    sizes, rhs_hbm, coef_hbm, mass_hbm, smoother_hbm, lift_hbm, restrict_hbm, cbm_hbm, label_hbm,
    out_ref,
    rhs, mass, smoother, lift, restrict, cbm, coef, label,
    dcol, onehot, pick, u, first, tr, faces, v, lsg, wide, scatter, s_off, m_hi, m_lo,
    out_a, in_a, out_z, in_z, c, out_by, out_bz, in_bx, in_by, in_bz, zone_out, in_zone,
    load_sem, sa, ra, sb, rb, sz, rz,
):
    ngx, ngy, ngz = sizes
    places = [lax.axis_index(axis) for axis in ("gx", "gy", "gz")]

    def along(dim, step):
        size = sizes[dim]
        return {("gx", "gy", "gz")[dim]: lax.rem(places[dim] + (step + size), size)}

    beside = [(along(dim, 1), along(dim, -1)) for dim in range(3)]
    there = [(places[dim] < sizes[dim] - 1, places[dim] > 0) for dim in range(3)]
    line = [along(0, step) for step in range(1, ngx)]

    barrier = pltpu.get_barrier_semaphore()
    partners = ngx - 1
    for dim in (2, 1):
        for way in (0, 1):
            partners = partners + jnp.where(there[dim][way], 1, 0)

            @pl.when(there[dim][way])
            def _():
                pl.semaphore_signal(barrier, inc=1, device_id=beside[dim][way], device_id_type=MESH)
    for device in line:
        pl.semaphore_signal(barrier, inc=1, device_id=device, device_id_type=MESH)

    loads = [
        pltpu.make_async_copy(src, dst, load_sem.at[n])
        for n, (src, dst) in enumerate(
            [
                (coef_hbm, coef),
                (label_hbm, label),
                (rhs_hbm, rhs),
                (smoother_hbm, smoother),
                (restrict_hbm, restrict),
                (cbm_hbm, cbm),
                (mass_hbm, mass),
                (lift_hbm.at[FACE : 2 * FACE], lift.at[0:FACE]),
                (lift_hbm.at[0:FACE], lift.at[FACE : 2 * FACE]),
                (lift_hbm.at[2 * FACE :], lift.at[2 * FACE :]),
            ]
        )
    ]
    for copy in loads:
        copy.start()

    class Message:
        def __init__(self, src, dst, send_sem, recv_sem, device, goes, comes):
            self.copy = pltpu.make_async_remote_copy(
                src_ref=src, dst_ref=dst, send_sem=send_sem, recv_sem=recv_sem,
                device_id=device, device_id_type=MESH,
            )
            self.goes, self.comes = goes, comes

        def start(self):
            self.when(self.goes, self.copy.start)
            return self

        def wait_recv(self):
            self.when(self.comes, self.copy.wait_recv)

        def wait_send(self):
            self.when(self.goes, self.copy.wait_send)

        def when(self, condition, act):
            if condition is None:
                act()
            else:
                pl.when(condition)(act)

    def shifted(dim, way, src, dst, send_sem, recv_sem):
        return Message(src, dst, send_sem, recv_sem, beside[dim][way], there[dim][way], there[dim][1 - way])

    for dim in range(3):
        for way in (0, 1):

            @pl.when(jnp.logical_not(there[dim][1 - way]))
            def _():
                if dim < 2:
                    in_a[2 * dim + way] = jnp.zeros((FACE, 128), F32)
                else:
                    in_z[way] = jnp.zeros((16, 128), F32)
                if dim == 0:
                    in_bx[way] = jnp.zeros((8, 128), F32)
                elif dim == 1:
                    in_by[way] = jnp.zeros((8, 128), F32)
                else:
                    in_bz[way] = jnp.zeros((16, 128), F32)
                if dim > 0:
                    in_zone[ngx - 1 + 2 * (dim - 1) + way] = jnp.zeros((8, 128), F32)

    node, face = iota((N, 256), 0), iota((N, 256), 1)
    block, within = face // FACE, face % FACE
    hi, lo = within // 8, within % 8
    end = jnp.where(block % 2 == 0, 7, 0)
    wanted = jnp.where(block < 2, hi * 64 + end * 8 + lo, hi * 64 + lo * 8 + end)
    pick[...] = jnp.where(node == wanted, 1.0, 0.0).astype(BF16)

    lane = iota((32, 128), 1)
    row = iota((32, 128), 0)

    def column(values):
        return jnp.sum(jnp.where(lane == row, jnp.broadcast_to(values, (32, 128)), 0.0), 1, keepdims=True)

    loads[0].wait()
    loads[1].wait()
    pad = jnp.zeros((1, 96), F32)
    for s in range(16):
        values = jnp.concatenate([coef[s // 4, s % 4 : s % 4 + 1, :], pad], 1)
        dcol[32 * s : 32 * s + 32, :] = jnp.broadcast_to(1.0 / column(values), (32, 128))
        names = jnp.concatenate([label[s // 4, s % 4 : s % 4 + 1, :].astype(F32), pad], 1)
        names = jnp.broadcast_to(column(names), (32, 128)).astype(jnp.int32)
        onehot[32 * s : 32 * s + 32, :] = jnp.where(names == lane % 64, 1.0, 0.0)
    d4 = lambda a: jnp.concatenate([a] * 4, 1)

    loads[2].wait()
    loads[3].wait()
    u[...] = dot3(rhs[...], smoother[...])
    first[...] = u[...] * d4(dcol[...])

    low = iota((FACE, 128), 1) < FACE
    swap = lambda a: pltpu.roll(a, FACE, 1)
    top, bottom = first[384:512, 384:512], first[0:128, 0:128]
    out_a[0] = jnp.where(low, swap(top[0:64]), top[64:128])
    out_a[1] = jnp.where(low, bottom[0:64], swap(bottom[64:128]))
    f_hi, f_lo = halves(first[...])
    tr[...] = dot1(f_hi, pick[...]) + dot1(f_lo, pick[...])
    ytop = [tr[128 * i + 96 : 128 * i + 128, 0:128] for i in range(4)]
    ybottom = [tr[128 * i : 128 * i + 32, 0:128] for i in range(4)]
    out_a[2] = jnp.where(low, jnp.concatenate(ytop[:2], 0), swap(jnp.concatenate(ytop[2:], 0)))
    out_a[3] = jnp.where(low, swap(jnp.concatenate(ybottom[:2], 0)), jnp.concatenate(ybottom[2:], 0))
    for i in range(16):
        out_z[0, i : i + 1, :] = tr[32 * i + 31 : 32 * i + 32, 128:256]
        out_z[1, i : i + 1, :] = tr[32 * i : 32 * i + 1, 128:256]
    pl.semaphore_wait(barrier, partners)
    z_traces = [
        shifted(2, way, out_z.at[way], in_z.at[way], sa.at[4 + way], ra.at[4 + way]).start()
        for way in (0, 1)
    ]
    a_copies = [
        shifted(dim, way, out_a.at[2 * dim + way], in_a.at[2 * dim + way], sa.at[2 * dim + way], ra.at[2 * dim + way]).start()
        for dim in (1, 0)
        for way in (0, 1)
    ]

    for copy in loads[4:]:
        copy.wait()

    lane_n = iota((N, 128), 1)
    first_half = lane_n < 64

    def table(a):
        hi, lo = halves(a)
        top = first_half[0 : a.shape[0]]
        return jnp.where(top, hi, lo), jnp.where(top, hi, jnp.zeros_like(hi))

    def project(a, columns):
        hi, lo = halves(a)
        t = dot1(hi, columns[0]) + dot1(lo, columns[1])
        return t + swap(t)

    many = jnp.concatenate([restrict[...]] * 16, 0)
    block = iota((384, 128), 0) // FACE
    kind = (iota((384, 128), 1) % 64) // 8
    r_wide = many.T
    r_table = table(r_wide)
    lift_r = jnp.where(kind == jnp.where(block < 5, block + 1, 7), project(lift[...], r_table), 0.0)
    unit = jnp.where(iota((128, 128), 0) == iota((128, 128), 1), 1.0, 0.0)
    m_hi[...], m_lo[...] = halves(mass[...])
    for i in range(4):
        part = slice(128 * i, 128 * i + 128)
        m_hi[part, part], m_lo[part, part] = halves(mass[part, part] - unit)

    def mass_rest(columns):
        t = dot1(m_hi[...], columns[0]) + dot1(m_lo[...], columns[1])
        return t + swap(t)

    scatter[...] = jnp.where(lane_n % 64 < 8, -(r_wide + mass_rest(r_table)), 0.0)
    scatter[0:64, :] = scatter[0:64, :] + lift_r[0:64]
    scatter[448:512, :] = scatter[448:512, :] + lift_r[64:128]
    for i in range(8):
        for j, at in ((7, 128), (0, 192)):
            rows = slice(64 * i + 8 * j, 64 * i + 8 * j + 8)
            scatter[rows, :] = scatter[rows, :] + lift_r[at + 8 * i : at + 8 * i + 8]
    for k, at in ((7, 256), (0, 320)):
        rows = pl.ds(k, FACE, stride=8)
        scatter[rows, :] = scatter[rows, :] + lift_r[at : at + FACE]
    g = scatter[...]

    s_off[...] = smoother[...].astype(BF16)
    for i in range(4):
        part = slice(128 * i, 128 * i + 128)
        s_off[part, part] = (smoother[part, part] - unit).astype(BF16)
    t = dot1(s_off[...], table(g)[0])
    s_rest = t + swap(t)
    sg = g + s_rest
    sg_table = table(sg)
    lsg[...] = project(lift[...], sg_table)
    l_table = table(lsg[...])
    small_g = -(s_rest + mass_rest(sg_table))
    own = jnp.where(lane_n % 64 < 8, r_wide, 0.0)
    t = dot1(u[...].astype(BF16), table(small_g)[0])
    wide[...] = project(rhs[...], table(sg + own)) + (t + swap(t))
    weight = 1.0 + jnp.sum(onehot[...], 0, keepdims=True)
    weight = jnp.broadcast_to(weight, (8, 128))
    per = 1.0 / weight
    d_row = 1.0 / jnp.concatenate([coef[s // 4, s % 4 : s % 4 + 1, :] for s in range(16)], 1)

    low32 = lane < FACE
    nothing = jnp.zeros((32, 128), F32)
    for s in range(16):
        x, y = s // 4, s % 4
        rows = slice(32 * s, 32 * s + 32)
        above = first[32 * s + 128 : 32 * s + 160, 0:128] if x < 3 else nothing
        below = first[32 * s - 128 : 32 * s - 96, 384:512] if x > 0 else nothing
        faces[rows, 0:128] = jnp.where(low32, above, below)
        above = tr[32 * s + 32 : 32 * s + 64, 0:128] if y < 3 else nothing
        below = tr[32 * s - 32 : 32 * s, 0:128] if y > 0 else nothing
        faces[rows, 128:256] = jnp.where(low32, below, above)
        own = tr[rows, 128:256]
        below = jnp.where(row == 0, 0.0, pltpu.roll(own, 1, 0))
        above = jnp.where(row == 31, 0.0, pltpu.roll(own, 31, 0))
        faces[rows, 256:384] = jnp.where(low32, below, above)

    wide[...] = wide[...] + project(faces[...], l_table)
    low16 = iota((16, 128), 1) < FACE
    ends = jnp.concatenate([jnp.where(low16, out_z[0], 0.0), jnp.where(low16, 0.0, out_z[1])], 0)
    back = dot3(ends, lsg[256:384, :])
    none64 = jnp.zeros((FACE, 128), BF16)

    def twice(a):
        return jnp.concatenate([jnp.concatenate([a, none64], 1), jnp.concatenate([none64, a], 1)], 0)

    packed_table = [[twice(part[at : at + FACE]) for part in l_table] for at in (64, 0, 128, 192)]

    for copy in a_copies:
        copy.wait_recv()
    for n in range(4):
        hi, lo = halves(in_a[n])
        t = dot1(hi, packed_table[n][0]) + dot1(lo, packed_table[n][1])
        parts = [t[:, 0:128] + swap(t[:, 0:128]), t[:, 128:256] + swap(t[:, 128:256])]
        for i in range(4):
            part = parts[i // 2][32 * (i % 2) : 32 * (i % 2) + 32]
            at = (32 * i, 384 + 32 * i, 128 * i, 128 * i + 96)[n]
            wide[at : at + 32, :] = wide[at : at + 32, :] + part
    lane16 = iota((16, 128), 1)
    for way, at in ((0, 31), (1, 0)):
        d_ends = dcol[pl.ds(at, 16, stride=32), :]
        out_bz[way] = jnp.where(lane16 // 8 == 6, d_ends, d_ends * wide[pl.ds(at, 16, stride=32), :])
    z_ways = [
        shifted(2, way, out_bz.at[way], in_bz.at[way], sb.at[4 + way], rb.at[4 + way]).start() for way in (0, 1)
    ]

    for copy in z_traces:
        copy.wait_recv()
    ends = jnp.concatenate([jnp.where(low16, in_z[0], 0.0), jnp.where(low16, 0.0, in_z[1])], 0)
    more = dot3(ends, lsg[256:384, :])
    wide[pl.ds(0, 16, stride=32), :] = wide[pl.ds(0, 16, stride=32), :] + more[0:16]
    wide[pl.ds(31, 16, stride=32), :] = wide[pl.ds(31, 16, stride=32), :] + more[16:32]
    w = wide[...].T
    c[...] = jnp.concatenate([w[0:8], w[8:64] * d_row], 0)
    quarter = iota((8, 128), 1) // 32

    def gather_y(tiles, turns):
        packed = jnp.zeros((8, 128), F32)
        for i in range(4):
            packed = jnp.where(quarter == i, pltpu.roll(tiles[i], turns[i], 1), packed)
        return packed

    out_by[0] = gather_y([c[24:32, 128 * i : 128 * i + 128] for i in range(4)], [32, 64, 96, 0])
    out_by[1] = gather_y([c[32:40, 128 * i : 128 * i + 128] for i in range(4)], [0, 32, 64, 96])

    b_copies = [
        shifted(0, 0, c.at[16:24, 384:512], in_bx.at[0], sb.at[0], rb.at[0]).start(),
        shifted(0, 1, c.at[8:16, 0:128], in_bx.at[1], sb.at[1], rb.at[1]).start(),
        shifted(1, 0, out_by.at[0], in_by.at[0], sb.at[2], rb.at[2]).start(),
        shifted(1, 1, out_by.at[1], in_by.at[1], sb.at[3], rb.at[3]).start(),
    ] + z_ways

    faces[0:64, 0:128] = jnp.where(low, faces[0:64, 0:128], swap(in_a[0]))
    faces[64:128, 0:128] = jnp.where(low, faces[64:128, 0:128], in_a[0])
    faces[384:448, 0:128] = jnp.where(low, in_a[1], faces[384:448, 0:128])
    faces[448:512, 0:128] = jnp.where(low, swap(in_a[1]), faces[448:512, 0:128])
    for i in range(4):
        half = slice(32 * (i % 2), 32 * (i % 2) + 32)
        below, above = in_a[2, half, :], in_a[3, half, :]
        below = below if i < 2 else swap(below)
        above = swap(above) if i < 2 else above
        j = 128 * i
        faces[j : j + 32, 128:256] = jnp.where(low32, below, faces[j : j + 32, 128:256])
        j = 128 * i + 96
        faces[j : j + 32, 128:256] = jnp.where(low32, faces[j : j + 32, 128:256], above)

    for s in range(16):
        at = 32 * s
        faces[at : at + 1, 256:384] = jnp.where(lane[0:1] < FACE, in_z[0, s : s + 1, :], faces[at : at + 1, 256:384])
        at = 32 * s + 31
        faces[at : at + 1, 256:384] = jnp.where(lane[0:1] < FACE, faces[at : at + 1, 256:384], in_z[1, s : s + 1, :])
    u_hi, u_lo = halves(u[...])
    v[...] = rhs[...] - (u[...] + (dot1(u_hi, m_hi[...]) + dot1(u_lo, m_hi[...]) + dot1(u_hi, m_lo[...])))

    small = c[0:8, :]
    none8 = jnp.zeros((8, 128), F32)
    place = iota((8, N), 1)
    py, pz = (place // 32) % 4, place % 32
    small = small + jnp.concatenate([c[8:16, 128:512], none8], 1)
    small = small + jnp.concatenate([none8, c[16:24, 0:384]], 1)
    small = small + jnp.where(py > 0, pltpu.roll(c[24:32, :], 32, 1), 0.0)
    small = small + jnp.where(py < 3, pltpu.roll(c[32:40, :], N - 32, 1), 0.0)
    small = small + jnp.where(pz > 0, pltpu.roll(c[40:48, :], 1, 1), 0.0)
    small = small + jnp.where(pz < 31, pltpu.roll(c[56:64, :], N - 1, 1), 0.0)
    one = onehot[...].astype(BF16)
    z_names = [onehot[pl.ds(0, 16, stride=32), :], onehot[pl.ds(31, 16, stride=32), :]]
    z_names = jnp.concatenate(z_names * 2, 0).astype(BF16)
    r_hi, r_lo = halves(restrict[...])
    r_hi, r_lo = r_hi.astype(F32), r_lo.astype(F32)
    r_stack = jnp.concatenate([r_hi, r_hi, r_lo], 0).astype(BF16)

    for copy in b_copies:
        copy.wait_recv()
    zeros_mid = jnp.zeros((8, 256), F32)
    small = small + jnp.concatenate([in_bx[0], zeros_mid, in_bx[1]], 1)
    below = [jnp.where(quarter == 0, pltpu.roll(in_by[0], turn, 1), 0.0) for turn in (0, 96, 64, 32)]
    above = [jnp.where(quarter == 3, pltpu.roll(in_by[1], turn, 1), 0.0) for turn in (96, 64, 32, 0)]
    small = small + jnp.concatenate([a + b for a, b in zip(below, above)], 1)
    z_low = in_bz[0] + pltpu.roll(in_bz[0], 120, 1) * back[16:32]
    z_high = in_bz[1] + pltpu.roll(in_bz[1], 8, 1) * back[0:16]
    z_add = jnp.concatenate([jnp.where(lane16 // 8 == 5, z_low, 0.0), jnp.where(lane16 // 8 == 7, z_high, 0.0)], 0)
    n_hi, n_lo = halves(z_add)
    z_add = jnp.concatenate([n_hi.astype(F32), n_lo.astype(F32)], 0).astype(BF16)
    z_add = lax.dot_general(z_add, z_names, TN, preferred_element_type=F32)
    q_hi, q_lo = halves(small)
    parts = dot1(jnp.concatenate([q_hi.astype(F32), q_lo.astype(F32)], 0).astype(BF16), one)
    coarse_rhs = parts[0:8] + parts[8:16] + (z_add[40:48] + z_add[56:64])
    zone = coarse_rhs * per
    zone_out[...] = zone

    z_copies = []
    for dim in (2, 1):
        for way in (0, 1):
            n = ngx - 1 + 2 * (dim - 1) + way
            z_copies.append(shifted(dim, way, zone_out, in_zone.at[n], sz.at[n], rz.at[n]).start())
    z_copies += [
        Message(zone_out, in_zone.at[n], sz.at[n], rz.at[n], device, None, None).start()
        for n, device in enumerate(line)
    ]

    v[...] = v[...] + dot3(faces[...], lift[...])
    first[...] = (u[...] + dot3(v[...], smoother[...])) * d4(dcol[...])
    two = zone + (coarse_rhs - (weight * dot3(cbm[...], zone) - zone)) * per

    for copy in z_copies:
        copy.wait_recv()
    total = in_zone[0]
    for n in range(1, ngx + 3):
        total = total + in_zone[n]
    two = two + total * per
    t_hi, t_lo = halves(two)
    t_hi, t_lo = t_hi.astype(F32), t_lo.astype(F32)
    t_stack = jnp.concatenate([t_hi, t_lo, t_hi], 0).astype(BF16)
    spread = lax.dot_general(t_stack, r_stack, TN, preferred_element_type=F32)
    e_hi, e_lo = halves(spread)
    spread = jnp.where(iota((128, N), 0) < 64, e_hi, e_lo)
    out_ref[...] = first[...] + dot1(one, spread)

    for copy in z_traces + a_copies + b_copies + z_copies:
        copy.wait_send()


def shards(sizes, rhs, coef, mass, smoother, lift, restrict, coarse_block_matrix, element_cluster_index):
    others = sizes[0] - 1 + 4
    hbm = pl.BlockSpec(memory_space=pl.ANY)
    dma = pltpu.SemaphoreType.DMA
    out = pl.pallas_call(
        functools.partial(kernel, sizes),
        out_shape=pltpu.VMEM((N, N), F32),
        in_specs=[hbm] * 8,
        out_specs=pl.BlockSpec(memory_space=pltpu.VMEM),
        scratch_shapes=[
            pltpu.VMEM((N, N), F32),
            pltpu.VMEM((N, N), F32),
            pltpu.VMEM((N, N), F32),
            pltpu.VMEM((384, N), F32),
            pltpu.VMEM((8, N), F32),
            pltpu.VMEM((8, 8), F32),
            pltpu.VMEM((4, 4, 32), F32),
            pltpu.VMEM((4, 4, 32), jnp.int32),
            pltpu.VMEM((N, 128), F32),
            pltpu.VMEM((N, 128), F32),
            pltpu.VMEM((N, 256), BF16),
            pltpu.VMEM((N, N), F32),
            pltpu.VMEM((N, N), F32),
            pltpu.VMEM((N, 256), F32),
            pltpu.VMEM((N, 384), F32),
            pltpu.VMEM((N, N), F32),
            pltpu.VMEM((384, 128), F32),
            pltpu.VMEM((N, 128), F32),
            pltpu.VMEM((N, 128), F32),
            pltpu.VMEM((N, N), BF16),
            pltpu.VMEM((N, N), BF16),
            pltpu.VMEM((N, N), BF16),
            pltpu.VMEM((4, FACE, 128), F32),
            pltpu.VMEM((4, FACE, 128), F32),
            pltpu.VMEM((2, 16, 128), F32),
            pltpu.VMEM((2, 16, 128), F32),
            pltpu.VMEM((FACE, N), F32),
            pltpu.VMEM((2, 8, 128), F32),
            pltpu.VMEM((2, 16, 128), F32),
            pltpu.VMEM((2, 8, 128), F32),
            pltpu.VMEM((2, 8, 128), F32),
            pltpu.VMEM((2, 16, 128), F32),
            pltpu.VMEM((8, 128), F32),
            pltpu.VMEM((others, 8, 128), F32),
            dma((10,)),
            dma((6,)),
            dma((6,)),
            dma((6,)),
            dma((6,)),
            dma((others,)),
            dma((others,)),
        ],
        compiler_params=pltpu.CompilerParams(
            collective_id=0, has_side_effects=True, vmem_limit_bytes=40 * 1024 * 1024
        ),
        name="cycle",
    )(*[
        pltpu.with_memory_space_constraint(a, pltpu.HBM)
        for a in (rhs.reshape(N, N), coef, mass, smoother, lift, restrict.T, coarse_block_matrix, element_cluster_index)
    ])
    return out.reshape(rhs.shape)


def solution(mesh):
    sizes = tuple(mesh.shape[a] for a in ("gx", "gy", "gz"))
    return jax.shard_map(
        functools.partial(shards, sizes),
        mesh=mesh,
        in_specs=(
            P("gx", "gy", "gz", None),
            P("gx", "gy", "gz"),
            P(),
            P(),
            P(),
            P(),
            P(),
            P("gx", "gy", "gz"),
        ),
        out_specs=P("gx", "gy", "gz", None),
        check_vma=False,
    )
```
